256 devices in a mesh: ax: 32 (over x, y, core), th: 8 (over z).
Axes of the slice: x: 4, y: 4, z: 8, core: 2. Of those that a mesh axis runs over, the one named last changes fastest.
Arguments:
- populations: float32 [26, 16, 64, 4096], P(None, None, 'th', 'ax')
- wall_free: float32 [128, 262144], P(None, ('ax', 'th')), may hold values from 0 to 1
- wall_bound: float32 [128, 262144], P(None, ('ax', 'th')), may hold values from 0 to 0.5
- wall_propagator: float32 [128, 128], replicated
- bind_on: float32 [128], replicated, may hold values from 0.02 to 0.2
- bind_off: float32 [128], replicated, may hold values from 0.02 to 0.2
- iface_sector: int32 [262144, 1], P(('ax', 'th')), may hold values from 0 to 7; in each aligned block of 1024 rows (0 to 1023, 1024 to 2047, ...) at most 256 rows name the same one
- iface_line: int32 [262144], P(('ax', 'th')), may hold values from 0 to 1023
- strut_mask: int32 [262144], P(('ax', 'th')), may hold values 0 or 1
Outputs:
- drug_field: float32 [16, 64, 4096], P(None, 'th', 'ax')
- axial_flow: float32 [16, 64, 4096], P(None, 'th', 'ax')
- free_drug: float32 [128, 262144], P(None, ('ax', 'th'))
- bound_drug: float32 [128, 262144], P(None, ('ax', 'th'))
The draws below stay inside these ranges and needn't reach their ends.
Inputs may be any that keep to these rules, and one draw needn't show every extreme that they name: `iface_sector`: among the rows of one device at most 256 name one sector, and in some device exactly 256 do.
All inputs are finite; a program needn't handle non-finite values. No bound on the sum of `strut_mask` on one device may be relied on, other than what follows from the above.
Results may differ from the reference program's by a relative error of at most 0.00023.
Values sent between devices are 32-bit elements; how exact they have to be, the bound alone decides.
A program may use at most 64 MiB of HBM per device.

```python
import math
import jax
import jax.numpy as jnp
import numpy as np
from jax import lax

CR = 16
CS = 8
CZ = 128
WR = 128
STEPS = 4
SUB = 2
NS = 64
NZ = 4096
SURF = 1024
CAP = 256
LINES = 262144
N_AX = 32
N_TH = 8


DRAW_VELOCITIES = [(0, 0, 0), (1, 0, 0), (-1, 0, 0), (0, 1, 0), (0, -1, 0), (0, 0, 1), (0, 0, -1), (1, 1, 0), (-1, -1, 0), (1, -1, 0), (-1, 1, 0), (1, 0, 1), (-1, 0, -1), (1, 0, -1), (-1, 0, 1), (0, 1, 1), (0, -1, -1), (0, 1, -1), (0, -1, 1), (0, 0, 0), (1, 0, 0), (-1, 0, 0), (0, 1, 0), (0, -1, 0), (0, 0, 1), (0, 0, -1)]


DRAW_WEIGHTS = [1.0 / 3.0] + [1.0 / 18.0] * 6 + [1.0 / 36.0] * 12 + [0.25] + [0.125] * 6


def draw_populations(key, part):
    keys = jax.random.split(key, 6)
    shape = (CR, NS, NZ)
    density = 1.0 + 0.1 * jax.random.uniform(keys[0], shape, jnp.float32, -1.0, 1.0)
    speed_z = 0.05 + 0.06 * jax.random.uniform(keys[1], shape, jnp.float32, -1.0, 1.0)
    speed_s = 0.06 * jax.random.uniform(keys[2], shape, jnp.float32, -1.0, 1.0)
    speed_r = 0.05 * jax.random.uniform(keys[3], shape, jnp.float32, -1.0, 1.0)
    concentration = jnp.exp(jax.random.uniform(keys[4], shape, jnp.float32, -1.6, 0.7))
    members = []
    speed_sq = speed_z * speed_z + speed_s * speed_s + speed_r * speed_r
    for member in range(26):
        step_z, step_s, step_r = DRAW_VELOCITIES[member]
        projected = step_z * speed_z + step_s * speed_s + step_r * speed_r
        if member < 19:
            members.append(DRAW_WEIGHTS[member] * density * (1.0 + 3.0 * projected + 4.5 * projected * projected - 1.5 * speed_sq))
        else:
            members.append(DRAW_WEIGHTS[member] * concentration * (1.0 + 4.0 * projected))
    noise = 1.0 + 0.05 * jax.random.uniform(keys[5], (26,) + shape, jnp.float32, -1.0, 1.0)
    return jnp.stack(members) * noise


def draw_wall_propagator(key, part):
    keys = jax.random.split(key, 2)
    across = jnp.arange(WR, dtype=jnp.int32)
    diagonal_mask = across[:, None] == across[None, :]
    diagonal = jax.random.uniform(keys[0], (WR,), jnp.float32, 0.45, 0.6)
    spread = jax.random.uniform(keys[1], (WR, WR), jnp.float32, 0.0, 0.6 / (WR - 1))
    return jnp.where(diagonal_mask, diagonal[:, None], spread)


def set_ends(result, rng, least, top_value):
    place = [jax.random.randint(jax.random.fold_in(rng, axis), (), 0, length) for axis, length in enumerate(result.shape)]
    main_axis = result.shape.index(max(result.shape))
    next_to = place[:main_axis] + [(place[main_axis] + 1) % result.shape[main_axis]] + place[main_axis + 1:]
    return result.at[tuple(place)].set(least).at[tuple(next_to)].set(top_value)


def block_levels(own_key, shape, cuts, smallest, largest):
    level, own = 1.0, jax.random.fold_in(own_key, 6)
    for dim, parts in cuts:
        steps = jnp.exp(jax.random.uniform(jax.random.fold_in(own, dim), (parts,), jnp.float32, smallest / len(cuts), largest / len(cuts)))
        level = level * jnp.repeat(steps, shape[dim] // parts).reshape([-1 if axis == dim else 1 for axis in range(len(shape))])
    return level


def routed_block(key, own, number, rows, number_of, top, reach, skew):
    order = jax.random.permutation(key, number_of)
    crowded, usual = shares(number_of, rows * top, reach, skew, True), shares(number_of, rows * top, reach, skew, False)
    places = jnp.arange(number_of)

    def named(sizes, turn):
        used = int((sizes > 0).sum())
        fixed = max(1, used // 4)
        shifted = fixed + (places - fixed + turn * (used - fixed)) % max(1, number_of - fixed)
        return jnp.zeros((number_of,), jnp.int32).at[order[jnp.where(places < fixed, places, shifted)]].set(jnp.asarray(sizes, jnp.int32))

    sizes = jnp.where(number % 4 == 0, named(crowded, number // 4), named(usual, number - number // 4 - 1))
    mixed = jax.random.permutation(jax.random.fold_in(own, 3), number_of)
    source_of, sink = mixed[0:number_of // 2 * 2:2], mixed[1:number_of // 2 * 2:2]
    margin = jnp.minimum(sizes[source_of] - 1, reach - sizes[sink]) // 2
    margin = jnp.where((source_of == order[0]) | (sink == order[0]) | (sizes[sink] == 0), 0, jnp.maximum(margin, 0))
    shifted = jax.random.randint(jax.random.fold_in(own, 4), (number_of // 2,), 0, 1 << 20) % (margin + 1)
    sizes = sizes.at[source_of].add(-shifted).at[sink].add(shifted)
    labels = jnp.searchsorted(jnp.cumsum(sizes), jnp.arange(rows * top), side="right").astype(jnp.int32)
    listing = labels.reshape(top, rows).T
    listing = listing[jax.random.permutation(jax.random.fold_in(own, 1), rows)]
    turn = jax.random.randint(jax.random.fold_in(own, 2), (rows, 1), 0, top)
    return jnp.take_along_axis(listing, (jnp.arange(top)[None, :] + turn) % top, axis=1)


def shares(number_of, total, most, slope, full):
    loads = [(1 << 20) // math.isqrt(rank ** slope) + 1 for rank in range(1, number_of + 1)]
    largest = most if full else min(most, max(-(-total // number_of), total * loads[0] // sum(loads)))
    least = 1 if total - largest >= number_of - 1 else 0
    counts, rest = [largest] + [least] * (number_of - 1), total - largest - least * (number_of - 1)
    while rest > 0:
        free = [i for i in range(1, number_of) if counts[i] < largest] or [i for i in range(1, number_of) if counts[i] < most]
        whole, left = sum([loads[i] for i in free]), rest
        for i in free:
            addition = min(most - counts[i], max(1, left * loads[i] // whole), rest)
            counts[i] = counts[i] + addition
            rest = rest - addition
    return np.array(counts)


def setup_inputs(seed: int = 0) -> dict:
    splits = jax.random.split(jax.random.key(seed), 10)
    populations = draw_populations(jax.random.fold_in(splits[9], 71), 0)
    wall_free = jnp.clip(1.0 * jax.random.uniform(splits[1], (WR, LINES), jnp.float32) ** block_levels(splits[1], (WR, LINES), ((1, 256),), -0.2, 0.2), 0.0, 1.0)
    wall_bound = jnp.clip(0.5 * jax.random.uniform(splits[2], (WR, LINES), jnp.float32) ** block_levels(splits[2], (WR, LINES), ((1, 256),), -0.2, 0.2), 0.0, 0.5)
    wall_propagator = draw_wall_propagator(jax.random.fold_in(splits[9], 71), 0)
    bind_on = jnp.clip(jnp.exp(jax.random.uniform(splits[4], (WR,), jnp.float32, math.log(0.02), math.log(0.2))), 0.02, 0.2)
    bind_off = jnp.clip(jnp.exp(jax.random.uniform(splits[5], (WR,), jnp.float32, math.log(0.02), math.log(0.2))), 0.02, 0.2)
    iface_sector_keys = jax.random.split(jax.random.fold_in(splits[6], 1), LINES // SURF)
    iface_sector_turns = jax.random.permutation(jax.random.fold_in(splits[6], 3), LINES // SURF)
    iface_sector = jax.vmap(lambda own, number: routed_block(jax.random.fold_in(splits[6], 2), own, number, SURF, N_TH, 1, CAP, 2))(iface_sector_keys, iface_sector_turns).reshape((LINES, 1))
    iface_line = set_ends(jax.random.randint(splits[7], (LINES,), 0, SURF), jax.random.fold_in(splits[7], 1), 0, SURF - 1).astype(jnp.int32)
    strut_mask = set_ends((jax.random.randint(splits[8], (LINES,), 0, 4) < 1).astype(jnp.int32), jax.random.fold_in(splits[8], 1), 0, 1)
    return dict(populations=populations, wall_free=wall_free, wall_bound=wall_bound, wall_propagator=wall_propagator, bind_on=bind_on, bind_off=bind_off, iface_sector=iface_sector, iface_line=iface_line, strut_mask=strut_mask)


VELOCITIES = [(0, 0, 0), (1, 0, 0), (-1, 0, 0), (0, 1, 0), (0, -1, 0), (0, 0, 1), (0, 0, -1),
              (1, 1, 0), (-1, -1, 0), (1, -1, 0), (-1, 1, 0), (1, 0, 1), (-1, 0, -1), (1, 0, -1), (-1, 0, 1),
              (0, 1, 1), (0, -1, -1), (0, 1, -1), (0, -1, 1),
              (0, 0, 0), (1, 0, 0), (-1, 0, 0), (0, 1, 0), (0, -1, 0), (0, 0, 1), (0, 0, -1)]
WEIGHTS = [1.0 / 3.0] + [1.0 / 18.0] * 6 + [1.0 / 36.0] * 12 + [0.25] + [0.125] * 6
OPPOSITE = [0, 2, 1, 4, 3, 6, 5, 8, 7, 10, 9, 12, 11, 14, 13, 16, 15, 18, 17, 19, 21, 20, 23, 22, 25, 24]
MIRROR = [0, 1, 2, 3, 4, 6, 5, 7, 8, 9, 10, 13, 14, 11, 12, 17, 18, 15, 16, 19, 20, 21, 22, 23, 25, 24]
RELAX_FLOW = 1.25
RELAX_DRUG = 1.1
PUSH_AXIAL = 0.0001
PERMEABILITY = 0.3
RELEASE_RATE = 0.5


def collide(state):
    table = jnp.array(VELOCITIES, jnp.float32)
    weights = jnp.array(WEIGHTS, jnp.float32)[:, None, None, None]
    flow = state[:19]
    drug = state[19:]
    density = jnp.sum(flow, axis=0)
    momentum = jnp.einsum("qd,qabc->dabc", table[:19], flow, precision=lax.Precision.HIGHEST)
    momentum = momentum.at[0].add(PUSH_AXIAL)
    velocity = momentum / density
    projected = jnp.einsum("qd,dabc->qabc", table, velocity, precision=lax.Precision.HIGHEST)
    speed_sq = jnp.sum(velocity * velocity, axis=0)
    blood_proj = projected[:19]
    flow_eq = weights[:19] * density * (1.0 + 3.0 * blood_proj + 4.5 * blood_proj * blood_proj - 1.5 * speed_sq)
    concentration = jnp.sum(drug, axis=0)
    drug_eq = weights[19:] * concentration * (1.0 + 4.0 * projected[19:])
    return jnp.concatenate([flow - RELAX_FLOW * (flow - flow_eq), drug - RELAX_DRUG * (drug - drug_eq)], axis=0)


def stream_padded(padded, post):
    radial = post.shape[1]
    across = post.shape[2]
    along = post.shape[3]
    ghost = padded[:, 0:1][jnp.array(MIRROR, jnp.int32)]
    extended = jnp.concatenate([ghost, padded, jnp.zeros_like(ghost)], axis=1)
    portions = []
    for member in range(26):
        step_z, step_s, step_r = VELOCITIES[member]
        portion = extended[member, 1 - step_r:1 - step_r + radial, 1 - step_s:1 - step_s + across, 1 - step_z:1 - step_z + along]
        if step_r == -1:
            portion = portion.at[radial - 1].set(post[OPPOSITE[member], radial - 1])
        portions.append(portion)
    return jnp.stack(portions)


def wall_update(free, bound, source, strut_part, wall_propagator, bind_on, bind_off):
    free = free.at[0].add(source + RELEASE_RATE * strut_part)
    for substep in range(SUB):
        free = jnp.dot(wall_propagator, free, precision=lax.Precision.HIGHEST, preferred_element_type=jnp.float32)
        rate = bind_on[:, None] * free * (1.0 - bound) - bind_off[:, None] * bound
        free = free - rate
        bound = bound + rate
    return free, bound


def axial_momentum(state):
    table = jnp.array(VELOCITIES, jnp.float32)
    return jnp.einsum("q,qabc->abc", table[:19, 0], state[:19], precision=lax.Precision.HIGHEST)


def reference(populations, wall_free, wall_bound, wall_propagator, bind_on, bind_off, iface_sector, iface_line, strut_mask):
    drug_weights = jnp.array(WEIGHTS[19:], jnp.float32)[:, None, None]
    rows = jnp.arange(LINES, dtype=jnp.int32)
    slab = rows // (N_TH * SURF)
    target = ((slab * N_TH + iface_sector[:, 0]) * SURF + iface_line).astype(jnp.int32)
    strut_part = strut_mask.astype(jnp.float32)
    open_row = PERMEABILITY * (1.0 - strut_part[target])
    state, free, bound = populations, wall_free, wall_bound
    for round_index in range(STEPS):
        surface = jnp.sum(state[19:, CR - 1], axis=0)
        surface_rows = surface.reshape(N_TH, CS, N_AX, CZ).transpose(2, 0, 1, 3).reshape(LINES)
        flux = open_row * (surface_rows - free[0, target])
        source = jnp.zeros((LINES,), jnp.float32).at[target].add(flux)
        flux_field = flux.reshape(N_AX, N_TH, CS, CZ).transpose(1, 2, 0, 3).reshape(NS, NZ)
        free, bound = wall_update(free, bound, source, strut_part, wall_propagator, bind_on, bind_off)
        state = state.at[19:, CR - 1].add(-drug_weights * flux_field)
        post = collide(state)
        padded = jnp.pad(post, ((0, 0), (0, 0), (1, 1), (1, 1)), mode="wrap")
        state = stream_padded(padded, post)
    return jnp.sum(state[19:], axis=0), axial_momentum(state), free, bound
```

```python
import functools

import jax
import jax.numpy as jnp
from jax import lax
from jax.experimental import pallas as pl
from jax.experimental.pallas import tpu as pltpu
from jax.sharding import PartitionSpec as P

STEPS = 4
RELAX_FLOW = 1.25
RELAX_DRUG = 1.1
PUSH_AXIAL = 0.0001
PERMEABILITY = 0.3
RELEASE_RATE = 0.5

VELOCITIES = [
    (0, 0, 0), (1, 0, 0), (-1, 0, 0), (0, 1, 0), (0, -1, 0), (0, 0, 1), (0, 0, -1),
    (1, 1, 0), (-1, -1, 0), (1, -1, 0), (-1, 1, 0), (1, 0, 1), (-1, 0, -1),
    (1, 0, -1), (-1, 0, 1), (0, 1, 1), (0, -1, -1), (0, 1, -1), (0, -1, 1),
    (0, 0, 0), (1, 0, 0), (-1, 0, 0), (0, 1, 0), (0, -1, 0), (0, 0, 1), (0, 0, -1),
]
OPPOSITE = [0, 2, 1, 4, 3, 6, 5, 8, 7, 10, 9, 12, 11, 14, 13, 16, 15, 18, 17, 19, 21, 20, 23, 22, 25, 24]
MIRROR = [0, 1, 2, 3, 4, 6, 5, 7, 8, 9, 10, 13, 14, 11, 12, 17, 18, 15, 16, 19, 20, 21, 22, 23, 25, 24]

S_UP = [3, 7, 10, 15, 17, 22]
S_DOWN = [4, 8, 9, 16, 18, 23]
MOVING = S_UP + S_DOWN
STILL = [q for q in range(26) if q not in MOVING]
Z_UP = [1, 7, 9, 11, 13, 20]
Z_DOWN = [2, 8, 10, 12, 14, 21]

F32 = jnp.float32
BF16 = jnp.bfloat16
MESH = pl.DeviceIdType.MESH


def wait_bytes(ref, sem):
    pltpu.make_async_copy(ref, ref, sem).wait()


def kernel(
    pops, free_in, bound_in, prop, on_row, off_row, sector, line, strut,
    drug_out, axial_out, free, bound,
    moving, still, drug_top, drug_now, speed_top, packed, faces, tops,
    onehot_hi, onehot_lo, lanes_lo, code_in, open_row, line_open, line_count, line_strut,
    table, sums, fixed_out, fixed_in, source,
    wide, from_source, to_surface, on_wide, off_wide, substep, propagated,
    table_send, table_recv, sums_send, sums_recv, fixed_send, fixed_recv,
    flow_send, flow_recv, top_send, top_recv,
):
    n_ax, n_th = lax.axis_size("ax"), lax.axis_size("th")
    ax, th = lax.axis_index("ax"), lax.axis_index("th")
    radial = pops.shape[1]
    top = radial - 1
    lane = lax.broadcasted_iota(jnp.int32, (8, 128), 1)
    ax_up, ax_down = lax.rem(ax + 1, n_ax), lax.rem(ax + n_ax - 1, n_ax)
    th_up, th_down = lax.rem(th + 1, n_th), lax.rem(th + n_th - 1, n_th)

    def peer(offset):
        return (ax, lax.rem(th + offset, n_th))

    beside = [
        (ax_up, th), (ax_down, th),
        (ax_up, th_up), (ax_up, th_down), (ax_down, th_up), (ax_down, th_down),
    ]
    barrier = pltpu.get_barrier_semaphore()
    greeted = [peer(o) for o in range(1, n_th)] + beside
    for device in greeted:
        pl.semaphore_signal(barrier, inc=1, device_id=device, device_id_type=MESH)

    relative = lax.rem(sector[...] - th + n_th, n_th)
    line_all = line[...]
    line_lo = jnp.bitwise_and(line_all, 127)
    line_hi = jnp.right_shift(line_all, 7)
    code_out = relative * 8 + line_hi
    lanes_lo[...] = line_lo
    code_in[...] = lax.rem(n_th - relative, n_th) * 8 + line_hi
    n_blocks = 8 * n_th
    down_blocks = lax.broadcasted_iota(jnp.int32, (n_blocks, 128), 0)
    down_lanes = lax.broadcasted_iota(jnp.int32, (128, 128), 0)
    for s in range(8):
        part = pl.ds(128 * s, 128)
        onehot_hi[:, part] = jnp.where(down_blocks == code_out[s : s + 1, :], 1.0, 0.0).astype(BF16)
        onehot_lo[:, part] = jnp.where(down_lanes == line_lo[s : s + 1, :], 1.0, 0.0).astype(BF16)

    def by_line(values):
        high = values.astype(BF16).astype(F32)
        low = values - high
        total = None
        for s in range(0, 8, 2):
            part = pl.ds(128 * s, 256)
            ones = onehot_hi[:, part]
            rows = []
            for piece in (high, low):
                row = jnp.concatenate([piece[s : s + 1, :], piece[s + 1 : s + 2, :]], axis=1)
                rows.append(ones * row.astype(BF16))
            term = lax.dot_general(
                jnp.concatenate(rows, axis=0),
                onehot_lo[:, part],
                (((1,), (1,)), ((), ())),
                preferred_element_type=F32,
            )
            total = term if total is None else total + term
        return total[:n_blocks] + total[n_blocks:]

    def gathered(block):
        result = jnp.zeros((8, 128), F32)
        where = lanes_lo[...]
        code = code_in[...]
        for o in range(n_th):
            for hi in range(8):
                row = jnp.broadcast_to(block(o, hi), (8, 128))
                found = jnp.take_along_axis(row, where, axis=1, mode="promise_in_bounds")
                result = jnp.where(code == o * 8 + hi, found, result)
        return result

    def table_copy(t, o):
        return pltpu.make_async_remote_copy(
            table.at[t, 0], table.at[t, o], table_send.at[t], table_recv.at[t], peer(o), MESH
        )

    def sums_copy(t, o):
        return pltpu.make_async_remote_copy(
            sums.at[0, t, o], sums.at[1, t, o], sums_send.at[t], sums_recv.at[t], peer(o), MESH
        )

    def fixed_copy(o):
        return pltpu.make_async_remote_copy(
            fixed_out.at[o], fixed_in.at[o], fixed_send, fixed_recv, peer(o), MESH
        )

    def send_sums(t, surface):
        found = by_line(surface)
        for o in range(n_th):
            sums[0, t, o] = found[8 * o : 8 * o + 8]
        for o in range(1, n_th):
            sums_copy(t, o).start()

    for c in range(8):
        table[0, 0, c : c + 1, :] = free_in[0:1, 128 * c : 128 * c + 128]
    strut_own = strut[...].astype(F32)
    counts = by_line(jnp.ones((8, 128), F32))
    for o in range(n_th):
        fixed_out[o, 0] = strut_own
        fixed_out[o, 1] = counts[8 * o : 8 * o + 8]
    surface = pops[19, top]
    for q in range(20, 26):
        surface = surface + pops[q, top]
    for q in range(19, 26):
        drug_now[q - 19] = pops[q, top]
    drug_now[7] = surface
    pl.semaphore_wait(barrier, len(greeted))
    for o in range(1, n_th):
        fixed_copy(o).start()
        table_copy(0, o).start()
    send_sums(0, surface)

    prop_all = prop[...]
    prop_hi = prop_all.astype(BF16)
    prop_lo = (prop_all - prop_hi.astype(F32)).astype(BF16)
    wide[...] = jnp.concatenate([prop_hi, prop_lo, prop_hi], axis=1)
    from_source[...] = jnp.broadcast_to(prop_all[:, 0:1], (128, 128))
    to_surface[...] = jnp.transpose(jnp.broadcast_to(prop_all[0:1, :], (128, 128)))
    on_wide[...] = jnp.transpose(jnp.broadcast_to(on_row[...], (128, 128)))
    off_wide[...] = jnp.transpose(jnp.broadcast_to(off_row[...], (128, 128)))
    bound[...] = bound_in[...]
    WIDTH = 256
    LINES_OWN = free_in.shape[1]

    def diffuse(x):
        x_hi = x.astype(BF16)
        x_lo = (x - x_hi.astype(F32)).astype(BF16)
        return jnp.dot(
            wide[...], jnp.concatenate([x_hi, x_hi, x_lo], axis=0), preferred_element_type=F32
        )

    for c in range(0, LINES_OWN, WIDTH):
        propagated[:, c : c + WIDTH] = diffuse(free_in[:, c : c + WIDTH])

    def own(p, q, r):
        if q in S_UP:
            return moving.at[p, MOVING.index(q), r, 8:16, :]
        if q in S_DOWN:
            return moving.at[p, MOVING.index(q), r, 0:8, :]
        return still.at[p, STILL.index(q), r]

    def shifted_s(p, q, r):
        if q in S_UP:
            return moving[p, MOVING.index(q), r, 7:15, :]
        if q in S_DOWN:
            return moving[p, MOVING.index(q), r, 1:9, :]
        return still[p, STILL.index(q), r]

    def rotation(shift):
        return shift % 128 if isinstance(shift, int) else lax.rem(shift, 128)

    def pulled(t, p, q, r):
        value = shifted_s(p, q, r)
        step_z, step_s, _ = VELOCITIES[q]
        if step_z == 0:
            return value
        first = 8 - step_s
        if step_z == 1:
            face = faces[t, 0, first : first + 8, :]
            slot = Z_UP.index(q) * 16 + r
            face = pltpu.roll(face, rotation(128 - slot), 1)
            return jnp.where(lane == 0, face, pltpu.roll(value, 1, 1))
        face = faces[t, 1, first : first + 8, :]
        slot = Z_DOWN.index(q) * 16 + r
        face = pltpu.roll(face, rotation(127 - slot), 1)
        return jnp.where(lane == 127, face, pltpu.roll(value, 127, 1))

    def moved(t, p, q, r, where):
        step_r = VELOCITIES[q][2]
        if step_r == 1 and where == "bottom":
            return pulled(t, p, MIRROR[q], r)
        if step_r == -1 and where == "top":
            return own(p, OPPOSITE[q], r)[...]
        return pulled(t, p, q, r - step_r)

    def collide_flow(f):
        d = {q: f[q] - f[q + 1] for q in (1, 3, 5, 7, 9, 11, 13, 15, 17)}
        density = f[0]
        for q in range(1, 19):
            density = density + f[q]
        jz = d[1] + d[7] + d[9] + d[11] + d[13] + PUSH_AXIAL
        js = d[3] + d[7] - d[9] + d[15] + d[17]
        jr = d[5] + d[11] - d[13] + d[15] - d[17]
        uz, us, ur = jz / density, js / density, jr / density
        base = 1.0 - 1.5 * (uz * uz + us * us + ur * ur)
        edge = density * (RELAX_FLOW / 36.0)
        face = density * (RELAX_FLOW / 18.0)
        keep = 1.0 - RELAX_FLOW
        post = {0: keep * f[0] + density * (RELAX_FLOW / 3.0) * base}
        along = {
            1: uz, 3: us, 5: ur, 7: uz + us, 9: uz - us,
            11: uz + ur, 13: uz - ur, 15: us + ur, 17: us - ur,
        }
        for q, speed in along.items():
            weight = face if q < 7 else edge
            even = weight * (base + 4.5 * speed * speed)
            odd = weight * (3.0 * speed)
            post[q] = keep * f[q] + (even + odd)
            post[q + 1] = keep * f[q + 1] + (even - odd)
        return post, (uz, us, ur)

    def collide_drug(f, total, speeds):
        keep = 1.0 - RELAX_DRUG
        share = total * (RELAX_DRUG * 0.125)
        post = {19: keep * f[19] + 2.0 * share}
        for q, speed in zip((20, 22, 24), speeds):
            odd = 4.0 * speed
            post[q] = keep * f[q] + share * (1.0 + odd)
            post[q + 1] = keep * f[q + 1] + share * (1.0 - odd)
        return post

    def pack(post, r, packs):
        up, down = packs
        for k, q in enumerate(Z_UP):
            if q in post:
                slot = 16 * k + r
                up = jnp.where(lane == slot, pltpu.roll(post[q], rotation(slot + 1), 1), up)
        for k, q in enumerate(Z_DOWN):
            if q in post:
                slot = 16 * k + r
                down = jnp.where(lane == slot, pltpu.roll(post[q], rotation(slot), 1), down)
        return up, down

    def layer(read, p, r, packs, where):
        f = {q: read(q, r, where) for q in range(19 if where == "top" else 26)}
        post, speeds = collide_flow(f)
        if where == "top":
            for i in range(3):
                speed_top[i] = speeds[i]
        else:
            total = f[19]
            for q in range(20, 26):
                total = total + f[q]
            post.update(collide_drug(f, total, speeds))
        for q, value in post.items():
            own(p, q, r)[...] = value
        return pack(post, r, packs)

    def flow_copies(t, p):
        def copy(src, dst, device, i):
            return pltpu.make_async_remote_copy(
                src, dst, flow_send.at[t, i], flow_recv.at[t, i], device, MESH
            )

        up, down = (ax, th_up), (ax, th_down)
        copies = [
            copy(moving.at[p, 0:5, :, 15, :], moving.at[p, 0:5, :, 7, :], up, 0),
            copy(moving.at[p, 6:11, :, 0, :], moving.at[p, 6:11, :, 8, :], down, 1),
            copy(moving.at[p, 5, 0:top, 15, :], moving.at[p, 5, 0:top, 7, :], up, 2),
            copy(moving.at[p, 11, 0:top, 0, :], moving.at[p, 11, 0:top, 8, :], down, 3),
        ]
        for side, to in ((0, ax_up), (1, ax_down)):
            i = 4 + 3 * side
            copies += [
                copy(packed.at[t, side], faces.at[t, side, 8:16, :], (to, th), i),
                copy(packed.at[t, side, 7:8, :], faces.at[t, side, 7:8, :], (to, th_up), i + 1),
                copy(packed.at[t, side, 0:1, :], faces.at[t, side, 16:17, :], (to, th_down), i + 2),
            ]
        return copies

    def collide_all(t, p, read, bottom):
        packs = (jnp.zeros((8, 128), F32), jnp.zeros((8, 128), F32))
        if bottom:
            packs = layer(read, p, 0, packs, "bottom")
        packs = lax.fori_loop(
            1 if bottom else 0, top, lambda r, packs: layer(read, p, r, packs, "middle"), packs
        )
        up, down = layer(read, p, top, packs, "top")
        packed[t, 0] = up
        packed[t, 1] = down
        for copy in flow_copies(t, p):
            copy.start()

    def top_copies(t, p):
        def copy(src, dst, device, i):
            return pltpu.make_async_remote_copy(
                src, dst, top_send.at[t, i], top_recv.at[t, i], device, MESH
            )

        return [
            copy(drug_top.at[p, 1, 0:8, :], tops.at[t, 0], (ax_up, th), 0),
            copy(drug_top.at[p, 2, 0:8, :], tops.at[t, 1], (ax_down, th), 1),
            copy(drug_top.at[p, 3, 15, :], drug_top.at[p, 3, 7, :], (ax, th_up), 2),
            copy(drug_top.at[p, 4, 0, :], drug_top.at[p, 4, 8, :], (ax, th_down), 3),
        ]

    def wall_flux(t, p):
        wait_bytes(table.at[t, pl.ds(1, n_th - 1)], table_recv.at[t])
        free_rows = gathered(lambda o, hi: table[t, o, hi : hi + 1, :])
        surface = drug_now[7]
        flux = open_row[...] * (surface - free_rows)
        lowered = {19: drug_now[0] - 0.25 * flux}
        for q in range(20, 26):
            lowered[q] = drug_now[q - 19] - 0.125 * flux
        post = collide_drug(lowered, surface - flux, [speed_top[i] for i in range(3)])
        drug_top[p, 1, 0:8, :] = post[20]
        drug_top[p, 2, 0:8, :] = post[21]
        drug_top[p, 3, 8:16, :] = post[22]
        drug_top[p, 4, 0:8, :] = post[23]
        for copy in top_copies(t, p):
            copy.start()
        drug_top[p, 0, 0:8, :] = post[19]
        drug_top[p, 5, 0:8, :] = post[24]
        own(p, 25, top)[...] = post[25]

    def react(x, b, on, off):
        rate = on * x * (1.0 - b) - off * b
        return x - rate, b + rate

    def wall_first(t, send):
        wait_bytes(sums.at[1, t, pl.ds(1, n_th - 1)], sums_recv.at[t])
        total = sums[0, t, 0]
        for o in range(1, n_th):
            total = total + sums[1, t, o]
        flux = line_open[...] * (total - line_count[...] * table[t, 0])
        source[...] = flux + RELEASE_RATE * line_strut[...]
        for c in range(8):
            part = pl.ds(128 * c, 128)
            x = propagated[:, part] + from_source[...] * source[c : c + 1, :]
            x, b = react(x, bound[:, part], on_wide[...], off_wide[...])
            substep[:, part] = x
            bound[:, part] = b
            if send:
                x = jnp.sum(to_surface[...] * x, axis=0, keepdims=True)
                x, _ = react(x, b[0:1, :], on_wide[0:1, :], off_wide[0:1, :])
                table[t + 1, 0, c : c + 1, :] = x
        if send:
            for o in range(1, n_th):
                table_copy(t + 1, o).start()

    def wall_second(last):
        wide_on = jnp.concatenate([on_wide[...]] * (WIDTH // 128), axis=1)
        wide_off = jnp.concatenate([off_wide[...]] * (WIDTH // 128), axis=1)
        for c in range(0, LINES_OWN, WIDTH):
            part = pl.ds(c, WIDTH)
            x, b = react(diffuse(substep[:, part]), bound[:, part], wide_on, wide_off)
            bound[:, part] = b
            if last:
                free[:, part] = x
            else:
                propagated[:, part] = diffuse(x)

    def top_moved(t, p):
        f = {19: drug_top[p, 0, 0:8, :]}
        f[20] = jnp.where(lane == 0, pltpu.roll(tops[t, 0], 1, 1), pltpu.roll(drug_top[p, 1, 0:8, :], 1, 1))
        f[21] = jnp.where(lane == 127, pltpu.roll(tops[t, 1], 127, 1), pltpu.roll(drug_top[p, 2, 0:8, :], 127, 1))
        f[22] = drug_top[p, 3, 7:15, :]
        f[23] = drug_top[p, 4, 1:9, :]
        f[24] = own(p, 24, top - 1)[...]
        f[25] = drug_top[p, 5, 0:8, :]
        total = f[19]
        for q in range(20, 26):
            total = total + f[q]
        return f, total

    def wait_tops(t, p):
        for copy in top_copies(t, p):
            copy.wait()

    def wait_flow(t, p):
        for copy in flow_copies(t, p):
            copy.wait()

    def wait_coupling_sends(t):
        wait_bytes(table.at[t, pl.ds(1, n_th - 1)], table_send.at[t])
        wait_bytes(sums.at[1, t, pl.ds(1, n_th - 1)], sums_send.at[t])

    collide_all(0, 0, lambda q, r, where: pops[q, r], False)
    wait_bytes(fixed_in.at[pl.ds(1, n_th - 1)], fixed_recv)
    line_strut[...] = strut_own
    line_open[...] = PERMEABILITY * (1.0 - strut_own)
    count = fixed_out[0, 1]
    for o in range(1, n_th):
        count = count + fixed_in[o, 1]
    line_count[...] = count
    fixed_in[0, 0] = strut_own
    covered = gathered(lambda o, hi: fixed_in[o, 0, hi : hi + 1, :])
    open_row[...] = PERMEABILITY * (1.0 - covered)
    wait_bytes(fixed_in.at[pl.ds(1, n_th - 1)], fixed_send)

    def step(t, carry):
        p = lax.rem(t, 2)
        wall_flux(t, p)
        wall_first(t, True)
        wall_second(False)
        wait_coupling_sends(t)
        wait_flow(t, p)
        collide_all(t + 1, 1 - p, lambda q, r, where: moved(t, p, q, r, where), True)
        wait_tops(t, p)
        f, total = top_moved(t, p)
        for q in range(19, 26):
            drug_now[q - 19] = f[q]
        drug_now[7] = total
        send_sums(t + 1, total)
        return carry

    lax.fori_loop(0, STEPS - 1, step, 0)

    t, p = STEPS - 1, (STEPS - 1) % 2
    wall_flux(t, p)
    wait_flow(t, p)

    def result(r, where):
        f = {q: moved(t, p, q, r, where) for q in Z_UP[:5] + Z_DOWN[:5]}
        flow = None
        for q in Z_UP[:5]:
            term = f[q] - f[OPPOSITE[q]]
            flow = term if flow is None else flow + term
        axial_out[r] = flow
        if where != "top":
            total = moved(t, p, 19, r, where)
            for q in range(20, 26):
                total = total + moved(t, p, q, r, where)
            drug_out[r] = total

    def result_middle(r, carry):
        result(r, "middle")
        return carry

    result(0, "bottom")
    lax.fori_loop(1, top, result_middle, 0)
    result(top, "top")
    wall_first(t, False)
    wall_second(True)
    wait_coupling_sends(t)
    wait_tops(t, p)
    drug_out[top] = top_moved(t, p)[1]


def per_device(
    populations, wall_free, wall_bound, wall_propagator, bind_on, bind_off,
    iface_sector, iface_line, strut_mask,
):
    n_th = lax.axis_size("th")
    radial = populations.shape[1]
    vmem = pl.BlockSpec(memory_space=pltpu.VMEM)
    block = (8, 128)
    scratch = [
        pltpu.VMEM((2, len(MOVING), radial, 16, 128), F32),
        pltpu.VMEM((2, len(STILL), radial, 8, 128), F32),
        pltpu.VMEM((2, 6, 16, 128), F32),
        pltpu.VMEM((8, *block), F32),
        pltpu.VMEM((3, *block), F32),
        pltpu.VMEM((STEPS, 2, *block), F32),
        pltpu.VMEM((STEPS, 2, 24, 128), F32),
        pltpu.VMEM((STEPS, 2, *block), F32),
        pltpu.VMEM((8 * n_th, 1024), BF16),
        pltpu.VMEM((128, 1024), BF16),
        pltpu.VMEM(block, jnp.int32),
        pltpu.VMEM(block, jnp.int32),
        pltpu.VMEM(block, F32),
        pltpu.VMEM(block, F32),
        pltpu.VMEM(block, F32),
        pltpu.VMEM(block, F32),
        pltpu.VMEM((STEPS, n_th, *block), F32),
        pltpu.VMEM((2, STEPS, n_th, *block), F32),
        pltpu.VMEM((n_th, 2, *block), F32),
        pltpu.VMEM((n_th, 2, *block), F32),
        pltpu.VMEM(block, F32),
        pltpu.VMEM((128, 384), BF16),
        pltpu.VMEM((128, 128), F32),
        pltpu.VMEM((128, 128), F32),
        pltpu.VMEM((128, 128), F32),
        pltpu.VMEM((128, 128), F32),
        pltpu.VMEM((128, 1024), F32),
        pltpu.VMEM((128, 1024), F32),
        pltpu.SemaphoreType.DMA((STEPS,)),
        pltpu.SemaphoreType.DMA((STEPS,)),
        pltpu.SemaphoreType.DMA((STEPS,)),
        pltpu.SemaphoreType.DMA((STEPS,)),
        pltpu.SemaphoreType.DMA,
        pltpu.SemaphoreType.DMA,
        pltpu.SemaphoreType.DMA((STEPS, 10)),
        pltpu.SemaphoreType.DMA((STEPS, 10)),
        pltpu.SemaphoreType.DMA((STEPS, 4)),
        pltpu.SemaphoreType.DMA((STEPS, 4)),
    ]
    field = jax.ShapeDtypeStruct((radial, *block), F32)
    wall = jax.ShapeDtypeStruct(wall_free.shape, F32)
    return pl.pallas_call(
        kernel,
        out_shape=(field, field, wall, wall),
        in_specs=[vmem] * 9,
        out_specs=(vmem,) * 4,
        scratch_shapes=scratch,
        compiler_params=pltpu.CompilerParams(
            collective_id=0, has_side_effects=True, vmem_limit_bytes=40 * 2**20
        ),
    )(
        populations, wall_free, wall_bound, wall_propagator,
        bind_on.reshape(1, 128), bind_off.reshape(1, 128),
        iface_sector.reshape(block), iface_line.reshape(block), strut_mask.reshape(block),
    )


def solution(mesh):
    cells = P(None, "th", "ax")
    lines = P(None, ("ax", "th"))
    return jax.shard_map(
        per_device,
        mesh=mesh,
        in_specs=(
            P(None, None, "th", "ax"), lines, lines, P(), P(), P(),
            P(("ax", "th"), None), P(("ax", "th")), P(("ax", "th")),
        ),
        out_specs=(cells, cells, lines, lines),
        check_vma=False,
    )
```

```python
import functools

import jax
import jax.numpy as jnp
from jax import lax
from jax.experimental import pallas as pl
from jax.experimental.pallas import tpu as pltpu
from jax.sharding import PartitionSpec as P

STEPS = 4
RELAX_FLOW = 1.25
RELAX_DRUG = 1.1
PUSH_AXIAL = 0.0001
PERMEABILITY = 0.3
RELEASE_RATE = 0.5

VELOCITIES = [
    (0, 0, 0), (1, 0, 0), (-1, 0, 0), (0, 1, 0), (0, -1, 0), (0, 0, 1), (0, 0, -1),
    (1, 1, 0), (-1, -1, 0), (1, -1, 0), (-1, 1, 0), (1, 0, 1), (-1, 0, -1),
    (1, 0, -1), (-1, 0, 1), (0, 1, 1), (0, -1, -1), (0, 1, -1), (0, -1, 1),
    (0, 0, 0), (1, 0, 0), (-1, 0, 0), (0, 1, 0), (0, -1, 0), (0, 0, 1), (0, 0, -1),
]
OPPOSITE = [0, 2, 1, 4, 3, 6, 5, 8, 7, 10, 9, 12, 11, 14, 13, 16, 15, 18, 17, 19, 21, 20, 23, 22, 25, 24]
MIRROR = [0, 1, 2, 3, 4, 6, 5, 7, 8, 9, 10, 13, 14, 11, 12, 17, 18, 15, 16, 19, 20, 21, 22, 23, 25, 24]

S_UP = [3, 7, 10, 15, 17, 22]
S_DOWN = [4, 8, 9, 16, 18, 23]
MOVING = S_UP + S_DOWN
STILL = [q for q in range(26) if q not in MOVING]
Z_UP = [1, 7, 9, 11, 13, 20]
Z_DOWN = [2, 8, 10, 12, 14, 21]

F32 = jnp.float32
BF16 = jnp.bfloat16
MESH = pl.DeviceIdType.MESH


WIDTH = 256


def diffuse(wide, x):
    x_hi = x.astype(BF16)
    x_lo = (x - x_hi.astype(F32)).astype(BF16)
    return jnp.dot(
        wide[...], jnp.concatenate([x_hi, x_hi, x_lo], axis=0), preferred_element_type=F32
    )


def react(x, b, on, off):
    rate = on * x * (1.0 - b) - off * b
    return x - rate, b + rate


def wait_bytes(ref, sem):
    pltpu.make_async_copy(ref, ref, sem).wait()


def kernel(
    pops_hbm, free_hbm, bound_hbm, prop_hbm, on_hbm, off_hbm, sector_hbm, line_hbm, strut_hbm,
    drug_out, axial_out, substep, bound, wide, on_wide, off_wide,
    pops, free_in, prop, on_row, off_row, sector, line, strut, first_drug, first_free, load_sems,
    moving, still, drug_top, drug_now, speed_top, packed, faces, tops,
    onehot_hi, onehot_lo, lanes_lo, code_in, open_row, line_open, line_count, line_strut,
    table, sums, fixed_out, fixed_in, source,
    from_source, to_surface, propagated,
    table_send, table_recv, sums_send, sums_recv, fixed_send, fixed_recv,
    flow_send, flow_recv, top_send, top_recv,
):
    n_ax, n_th = lax.axis_size("ax"), lax.axis_size("th")
    ax, th = lax.axis_index("ax"), lax.axis_index("th")
    radial = pops.shape[1]
    top = radial - 1
    lane = lax.broadcasted_iota(jnp.int32, (8, 128), 1)
    ax_up, ax_down = lax.rem(ax + 1, n_ax), lax.rem(ax + n_ax - 1, n_ax)
    th_up, th_down = lax.rem(th + 1, n_th), lax.rem(th + n_th - 1, n_th)

    def peer(offset):
        return (ax, lax.rem(th + offset, n_th))

    beside = [
        (ax_up, th), (ax_down, th),
        (ax_up, th_up), (ax_up, th_down), (ax_down, th_up), (ax_down, th_down),
    ]
    barrier = pltpu.get_barrier_semaphore()
    greeted = [peer(o) for o in range(1, n_th)] + beside
    for device in greeted:
        pl.semaphore_signal(barrier, inc=1, device_id=device, device_id_type=MESH)

    loads = [
        (sector_hbm, sector), (line_hbm, line), (strut_hbm, strut),
        (pops_hbm.at[19:26, top], first_drug), (free_hbm.at[0:8, :], first_free),
        (prop_hbm, prop), (on_hbm, on_row), (off_hbm, off_row),
        (free_hbm, free_in), (pops_hbm, pops), (bound_hbm, bound),
    ]
    loads = [
        pltpu.make_async_copy(src, dst, load_sems.at[i]) for i, (src, dst) in enumerate(loads)
    ]
    for load in loads:
        load.start()
    for load in loads[:3]:
        load.wait()

    relative = lax.rem(sector[...] - th + n_th, n_th)
    line_all = line[...]
    line_lo = jnp.bitwise_and(line_all, 127)
    line_hi = jnp.right_shift(line_all, 7)
    code_out = relative * 8 + line_hi
    lanes_lo[...] = line_lo
    code_in[...] = lax.rem(n_th - relative, n_th) * 8 + line_hi
    n_blocks = 8 * n_th
    down_blocks = lax.broadcasted_iota(jnp.int32, (n_blocks, 128), 0)
    down_lanes = lax.broadcasted_iota(jnp.int32, (128, 128), 0)
    for s in range(8):
        part = pl.ds(128 * s, 128)
        onehot_hi[:, part] = jnp.where(down_blocks == code_out[s : s + 1, :], 1.0, 0.0).astype(BF16)
        onehot_lo[:, part] = jnp.where(down_lanes == line_lo[s : s + 1, :], 1.0, 0.0).astype(BF16)

    def by_line(values):
        high = values.astype(BF16).astype(F32)
        low = values - high
        total = None
        for s in range(0, 8, 2):
            part = pl.ds(128 * s, 256)
            ones = onehot_hi[:, part]
            rows = []
            for piece in (high, low):
                row = jnp.concatenate([piece[s : s + 1, :], piece[s + 1 : s + 2, :]], axis=1)
                rows.append(ones * row.astype(BF16))
            term = lax.dot_general(
                jnp.concatenate(rows, axis=0),
                onehot_lo[:, part],
                (((1,), (1,)), ((), ())),
                preferred_element_type=F32,
            )
            total = term if total is None else total + term
        return total[:n_blocks] + total[n_blocks:]

    def gathered(block):
        result = jnp.zeros((8, 128), F32)
        where = lanes_lo[...]
        code = code_in[...]
        for o in range(n_th):
            for hi in range(8):
                row = jnp.broadcast_to(block(o, hi), (8, 128))
                found = jnp.take_along_axis(row, where, axis=1, mode="promise_in_bounds")
                result = jnp.where(code == o * 8 + hi, found, result)
        return result

    def table_copy(t, o):
        return pltpu.make_async_remote_copy(
            table.at[t, 0], table.at[t, o], table_send.at[t], table_recv.at[t], peer(o), MESH
        )

    def sums_copy(t, o):
        return pltpu.make_async_remote_copy(
            sums.at[0, t, o], sums.at[1, t, o], sums_send.at[t], sums_recv.at[t], peer(o), MESH
        )

    def fixed_copy(o):
        return pltpu.make_async_remote_copy(
            fixed_out.at[o], fixed_in.at[o], fixed_send, fixed_recv, peer(o), MESH
        )

    def send_sums(t, surface):
        found = by_line(surface)
        for o in range(n_th):
            sums[0, t, o] = found[8 * o : 8 * o + 8]
        for o in range(1, n_th):
            sums_copy(t, o).start()

    for load in loads[3:5]:
        load.wait()
    for c in range(8):
        table[0, 0, c : c + 1, :] = first_free[0:1, 128 * c : 128 * c + 128]
    strut_own = strut[...].astype(F32)
    counts = by_line(jnp.ones((8, 128), F32))
    for o in range(n_th):
        fixed_out[o, 0] = strut_own
        fixed_out[o, 1] = counts[8 * o : 8 * o + 8]
    surface = first_drug[0]
    for q in range(20, 26):
        surface = surface + first_drug[q - 19]
    for q in range(19, 26):
        drug_now[q - 19] = first_drug[q - 19]
    drug_now[7] = surface
    pl.semaphore_wait(barrier, len(greeted))
    for o in range(1, n_th):
        fixed_copy(o).start()
        table_copy(0, o).start()
    send_sums(0, surface)

    for load in loads[5:]:
        load.wait()
    prop_all = prop[...]
    prop_hi = prop_all.astype(BF16)
    prop_lo = (prop_all - prop_hi.astype(F32)).astype(BF16)
    wide[...] = jnp.concatenate([prop_hi, prop_lo, prop_hi], axis=1)
    from_source[...] = jnp.broadcast_to(prop_all[:, 0:1], (128, 128))
    to_surface[...] = jnp.transpose(jnp.broadcast_to(prop_all[0:1, :], (128, 128)))
    on_wide[...] = jnp.transpose(jnp.broadcast_to(on_row[...], (128, 128)))
    off_wide[...] = jnp.transpose(jnp.broadcast_to(off_row[...], (128, 128)))
    n_lines = free_in.shape[1]
    for c in range(0, n_lines, WIDTH):
        propagated[:, c : c + WIDTH] = diffuse(wide, free_in[:, c : c + WIDTH])

    def own(p, q, r):
        if q in S_UP:
            return moving.at[p, MOVING.index(q), r, 8:16, :]
        if q in S_DOWN:
            return moving.at[p, MOVING.index(q), r, 0:8, :]
        return still.at[p, STILL.index(q), r]

    def shifted_s(p, q, r):
        if q in S_UP:
            return moving[p, MOVING.index(q), r, 7:15, :]
        if q in S_DOWN:
            return moving[p, MOVING.index(q), r, 1:9, :]
        return still[p, STILL.index(q), r]

    def rotation(shift):
        return shift % 128 if isinstance(shift, int) else lax.rem(shift, 128)

    def pulled(t, p, q, r):
        value = shifted_s(p, q, r)
        step_z, step_s, _ = VELOCITIES[q]
        if step_z == 0:
            return value
        first = 8 - step_s
        if step_z == 1:
            face = faces[t, 0, first : first + 8, :]
            slot = Z_UP.index(q) * 16 + r
            face = pltpu.roll(face, rotation(128 - slot), 1)
            return jnp.where(lane == 0, face, pltpu.roll(value, 1, 1))
        face = faces[t, 1, first : first + 8, :]
        slot = Z_DOWN.index(q) * 16 + r
        face = pltpu.roll(face, rotation(127 - slot), 1)
        return jnp.where(lane == 127, face, pltpu.roll(value, 127, 1))

    def moved(t, p, q, r, where):
        step_r = VELOCITIES[q][2]
        if step_r == 1 and where == "bottom":
            return pulled(t, p, MIRROR[q], r)
        if step_r == -1 and where == "top":
            return own(p, OPPOSITE[q], r)[...]
        return pulled(t, p, q, r - step_r)

    def collide_flow(f):
        d = {q: f[q] - f[q + 1] for q in (1, 3, 5, 7, 9, 11, 13, 15, 17)}
        density = f[0]
        for q in range(1, 19):
            density = density + f[q]
        jz = d[1] + d[7] + d[9] + d[11] + d[13] + PUSH_AXIAL
        js = d[3] + d[7] - d[9] + d[15] + d[17]
        jr = d[5] + d[11] - d[13] + d[15] - d[17]
        uz, us, ur = jz / density, js / density, jr / density
        base = 1.0 - 1.5 * (uz * uz + us * us + ur * ur)
        edge = density * (RELAX_FLOW / 36.0)
        face = density * (RELAX_FLOW / 18.0)
        keep = 1.0 - RELAX_FLOW
        post = {0: keep * f[0] + density * (RELAX_FLOW / 3.0) * base}
        along = {
            1: uz, 3: us, 5: ur, 7: uz + us, 9: uz - us,
            11: uz + ur, 13: uz - ur, 15: us + ur, 17: us - ur,
        }
        for q, speed in along.items():
            weight = face if q < 7 else edge
            even = weight * (base + 4.5 * speed * speed)
            odd = weight * (3.0 * speed)
            post[q] = keep * f[q] + (even + odd)
            post[q + 1] = keep * f[q + 1] + (even - odd)
        return post, (uz, us, ur)

    def collide_drug(f, total, speeds):
        keep = 1.0 - RELAX_DRUG
        share = total * (RELAX_DRUG * 0.125)
        post = {19: keep * f[19] + 2.0 * share}
        for q, speed in zip((20, 22, 24), speeds):
            odd = 4.0 * speed
            post[q] = keep * f[q] + share * (1.0 + odd)
            post[q + 1] = keep * f[q + 1] + share * (1.0 - odd)
        return post

    def pack(post, r, packs):
        up, down = packs
        for k, q in enumerate(Z_UP):
            if q in post:
                slot = 16 * k + r
                up = jnp.where(lane == slot, pltpu.roll(post[q], rotation(slot + 1), 1), up)
        for k, q in enumerate(Z_DOWN):
            if q in post:
                slot = 16 * k + r
                down = jnp.where(lane == slot, pltpu.roll(post[q], rotation(slot), 1), down)
        return up, down

    def layer(read, p, r, packs, where):
        f = {q: read(q, r, where) for q in range(19 if where == "top" else 26)}
        post, speeds = collide_flow(f)
        if where == "top":
            for i in range(3):
                speed_top[i] = speeds[i]
        else:
            total = f[19]
            for q in range(20, 26):
                total = total + f[q]
            post.update(collide_drug(f, total, speeds))
        for q, value in post.items():
            own(p, q, r)[...] = value
        return pack(post, r, packs)

    def flow_copies(t, p):
        def copy(src, dst, device, i):
            return pltpu.make_async_remote_copy(
                src, dst, flow_send.at[t, i], flow_recv.at[t, i], device, MESH
            )

        up, down = (ax, th_up), (ax, th_down)
        copies = [
            copy(moving.at[p, 0:5, :, 15, :], moving.at[p, 0:5, :, 7, :], up, 0),
            copy(moving.at[p, 6:11, :, 0, :], moving.at[p, 6:11, :, 8, :], down, 1),
            copy(moving.at[p, 5, 0:top, 15, :], moving.at[p, 5, 0:top, 7, :], up, 2),
            copy(moving.at[p, 11, 0:top, 0, :], moving.at[p, 11, 0:top, 8, :], down, 3),
        ]
        for side, to in ((0, ax_up), (1, ax_down)):
            i = 4 + 3 * side
            copies += [
                copy(packed.at[t, side], faces.at[t, side, 8:16, :], (to, th), i),
                copy(packed.at[t, side, 7:8, :], faces.at[t, side, 7:8, :], (to, th_up), i + 1),
                copy(packed.at[t, side, 0:1, :], faces.at[t, side, 16:17, :], (to, th_down), i + 2),
            ]
        return copies

    def collide_all(t, p, read, bottom):
        packs = (jnp.zeros((8, 128), F32), jnp.zeros((8, 128), F32))
        if bottom:
            packs = layer(read, p, 0, packs, "bottom")
        packs = lax.fori_loop(
            1 if bottom else 0, top, lambda r, packs: layer(read, p, r, packs, "middle"), packs
        )
        up, down = layer(read, p, top, packs, "top")
        packed[t, 0] = up
        packed[t, 1] = down
        for copy in flow_copies(t, p):
            copy.start()

    def top_copies(t, p):
        def copy(src, dst, device, i):
            return pltpu.make_async_remote_copy(
                src, dst, top_send.at[t, i], top_recv.at[t, i], device, MESH
            )

        return [
            copy(drug_top.at[p, 1, 0:8, :], tops.at[t, 0], (ax_up, th), 0),
            copy(drug_top.at[p, 2, 0:8, :], tops.at[t, 1], (ax_down, th), 1),
            copy(drug_top.at[p, 3, 15, :], drug_top.at[p, 3, 7, :], (ax, th_up), 2),
            copy(drug_top.at[p, 4, 0, :], drug_top.at[p, 4, 8, :], (ax, th_down), 3),
        ]

    def wall_flux(t, p):
        wait_bytes(table.at[t, pl.ds(1, n_th - 1)], table_recv.at[t])
        free_rows = gathered(lambda o, hi: table[t, o, hi : hi + 1, :])
        surface = drug_now[7]
        flux = open_row[...] * (surface - free_rows)
        lowered = {19: drug_now[0] - 0.25 * flux}
        for q in range(20, 26):
            lowered[q] = drug_now[q - 19] - 0.125 * flux
        post = collide_drug(lowered, surface - flux, [speed_top[i] for i in range(3)])
        drug_top[p, 1, 0:8, :] = post[20]
        drug_top[p, 2, 0:8, :] = post[21]
        drug_top[p, 3, 8:16, :] = post[22]
        drug_top[p, 4, 0:8, :] = post[23]
        for copy in top_copies(t, p):
            copy.start()
        drug_top[p, 0, 0:8, :] = post[19]
        drug_top[p, 5, 0:8, :] = post[24]
        own(p, 25, top)[...] = post[25]

    def wall_first(t, send):
        wait_bytes(sums.at[1, t, pl.ds(1, n_th - 1)], sums_recv.at[t])
        total = sums[0, t, 0]
        for o in range(1, n_th):
            total = total + sums[1, t, o]
        flux = line_open[...] * (total - line_count[...] * table[t, 0])
        source[...] = flux + RELEASE_RATE * line_strut[...]
        for c in range(8):
            part = pl.ds(128 * c, 128)
            x = propagated[:, part] + from_source[...] * source[c : c + 1, :]
            x, b = react(x, bound[:, part], on_wide[...], off_wide[...])
            substep[:, part] = x
            bound[:, part] = b
            if send:
                x = jnp.sum(to_surface[...] * x, axis=0, keepdims=True)
                x, _ = react(x, b[0:1, :], on_wide[0:1, :], off_wide[0:1, :])
                table[t + 1, 0, c : c + 1, :] = x
        if send:
            for o in range(1, n_th):
                table_copy(t + 1, o).start()

    def wall_second():
        wide_on = jnp.concatenate([on_wide[...]] * (WIDTH // 128), axis=1)
        wide_off = jnp.concatenate([off_wide[...]] * (WIDTH // 128), axis=1)
        for c in range(0, n_lines, WIDTH):
            part = pl.ds(c, WIDTH)
            x, b = react(diffuse(wide, substep[:, part]), bound[:, part], wide_on, wide_off)
            bound[:, part] = b
            propagated[:, part] = diffuse(wide, x)

    def top_moved(t, p):
        f = {19: drug_top[p, 0, 0:8, :]}
        f[20] = jnp.where(lane == 0, pltpu.roll(tops[t, 0], 1, 1), pltpu.roll(drug_top[p, 1, 0:8, :], 1, 1))
        f[21] = jnp.where(lane == 127, pltpu.roll(tops[t, 1], 127, 1), pltpu.roll(drug_top[p, 2, 0:8, :], 127, 1))
        f[22] = drug_top[p, 3, 7:15, :]
        f[23] = drug_top[p, 4, 1:9, :]
        f[24] = own(p, 24, top - 1)[...]
        f[25] = drug_top[p, 5, 0:8, :]
        total = f[19]
        for q in range(20, 26):
            total = total + f[q]
        return f, total

    def wait_tops(t, p):
        for copy in top_copies(t, p):
            copy.wait()

    def wait_flow(t, p):
        for copy in flow_copies(t, p):
            copy.wait()

    def wait_coupling_sends(t):
        wait_bytes(table.at[t, pl.ds(1, n_th - 1)], table_send.at[t])
        wait_bytes(sums.at[1, t, pl.ds(1, n_th - 1)], sums_send.at[t])

    collide_all(0, 0, lambda q, r, where: pops[q, r], False)
    wait_bytes(fixed_in.at[pl.ds(1, n_th - 1)], fixed_recv)
    line_strut[...] = strut_own
    line_open[...] = PERMEABILITY * (1.0 - strut_own)
    count = fixed_out[0, 1]
    for o in range(1, n_th):
        count = count + fixed_in[o, 1]
    line_count[...] = count
    fixed_in[0, 0] = strut_own
    covered = gathered(lambda o, hi: fixed_in[o, 0, hi : hi + 1, :])
    open_row[...] = PERMEABILITY * (1.0 - covered)
    wait_bytes(fixed_in.at[pl.ds(1, n_th - 1)], fixed_send)

    def wall_side(t, p):
        wait_tops(t, p)
        f, total = top_moved(t, p)
        for q in range(19, 26):
            drug_now[q - 19] = f[q]
        drug_now[7] = total
        send_sums(t + 1, total)

    def step(t, carry):
        p = lax.rem(t, 2)
        wall_flux(t, p)
        wall_first(t, True)
        pl.when(p == 1)(lambda: wall_side(t, p))
        wall_second()
        wait_coupling_sends(t)
        wait_flow(t, p)
        collide_all(t + 1, 1 - p, lambda q, r, where: moved(t, p, q, r, where), True)
        pl.when(p == 0)(lambda: wall_side(t, p))
        return carry

    lax.fori_loop(0, STEPS - 1, step, 0)

    t, p = STEPS - 1, (STEPS - 1) % 2
    wall_flux(t, p)
    wait_flow(t, p)

    def result(r, where):
        f = {q: moved(t, p, q, r, where) for q in Z_UP[:5] + Z_DOWN[:5]}
        flow = None
        for q in Z_UP[:5]:
            term = f[q] - f[OPPOSITE[q]]
            flow = term if flow is None else flow + term
        axial_out[r] = flow
        if where != "top":
            total = moved(t, p, 19, r, where)
            for q in range(20, 26):
                total = total + moved(t, p, q, r, where)
            drug_out[r] = total

    def result_middle(r, carry):
        result(r, "middle")
        return carry

    result(0, "bottom")
    lax.fori_loop(1, top, result_middle, 0)
    result(top, "top")
    wall_first(t, False)
    wait_coupling_sends(t)
    wait_tops(t, p)
    drug_out[top] = top_moved(t, p)[1]


def finish(
    substep, bound_in, wide, on_wide, off_wide, drug_in, axial_in,
    drug, axial, free, bound,
    free_part, bound_part, sems,
):
    copies = [
        pltpu.make_async_copy(drug_in, drug, sems.at[0]),
        pltpu.make_async_copy(axial_in, axial, sems.at[1]),
    ]
    for copy in copies:
        copy.start()
    wide_on = jnp.concatenate([on_wide[...]] * (WIDTH // 128), axis=1)
    wide_off = jnp.concatenate([off_wide[...]] * (WIDTH // 128), axis=1)
    for i in range(substep.shape[1] // WIDTH):
        part = pl.ds(i * WIDTH, WIDTH)
        x, b = react(diffuse(wide, substep[:, part]), bound_in[:, part], wide_on, wide_off)
        free_part[:, part] = x
        bound_part[:, part] = b
        for k, (src, dst) in enumerate(((free_part, free), (bound_part, bound))):
            copy = pltpu.make_async_copy(src.at[:, part], dst.at[:, part], sems.at[2 + 2 * i + k])
            copy.start()
            copies.append(copy)
    for copy in copies:
        copy.wait()


def per_device(
    populations, wall_free, wall_bound, wall_propagator, bind_on, bind_off,
    iface_sector, iface_line, strut_mask,
):
    n_th = lax.axis_size("th")
    radial = populations.shape[1]
    vmem = pl.BlockSpec(memory_space=pltpu.VMEM)
    hbm = pl.BlockSpec(memory_space=pltpu.HBM)
    block = (8, 128)
    wall_block = pltpu.VMEM(wall_free.shape, F32)
    scratch = [
        pltpu.VMEM(populations.shape, F32),
        wall_block,
        pltpu.VMEM((128, 128), F32),
        pltpu.VMEM((1, 128), F32),
        pltpu.VMEM((1, 128), F32),
        pltpu.VMEM(block, jnp.int32),
        pltpu.VMEM(block, jnp.int32),
        pltpu.VMEM(block, jnp.int32),
        pltpu.VMEM((7, *block), F32),
        pltpu.VMEM((8, wall_free.shape[1]), F32),
        pltpu.SemaphoreType.DMA((11,)),
        pltpu.VMEM((2, len(MOVING), radial, 16, 128), F32),
        pltpu.VMEM((2, len(STILL), radial, 8, 128), F32),
        pltpu.VMEM((2, 6, 16, 128), F32),
        pltpu.VMEM((8, *block), F32),
        pltpu.VMEM((3, *block), F32),
        pltpu.VMEM((STEPS, 2, *block), F32),
        pltpu.VMEM((STEPS, 2, 24, 128), F32),
        pltpu.VMEM((STEPS, 2, *block), F32),
        pltpu.VMEM((8 * n_th, 1024), BF16),
        pltpu.VMEM((128, 1024), BF16),
        pltpu.VMEM(block, jnp.int32),
        pltpu.VMEM(block, jnp.int32),
        pltpu.VMEM(block, F32),
        pltpu.VMEM(block, F32),
        pltpu.VMEM(block, F32),
        pltpu.VMEM(block, F32),
        pltpu.VMEM((STEPS, n_th, *block), F32),
        pltpu.VMEM((2, STEPS, n_th, *block), F32),
        pltpu.VMEM((n_th, 2, *block), F32),
        pltpu.VMEM((n_th, 2, *block), F32),
        pltpu.VMEM(block, F32),
        pltpu.VMEM((128, 128), F32),
        pltpu.VMEM((128, 128), F32),
        wall_block,
        pltpu.SemaphoreType.DMA((STEPS,)),
        pltpu.SemaphoreType.DMA((STEPS,)),
        pltpu.SemaphoreType.DMA((STEPS,)),
        pltpu.SemaphoreType.DMA((STEPS,)),
        pltpu.SemaphoreType.DMA,
        pltpu.SemaphoreType.DMA,
        pltpu.SemaphoreType.DMA((STEPS, 10)),
        pltpu.SemaphoreType.DMA((STEPS, 10)),
        pltpu.SemaphoreType.DMA((STEPS, 4)),
        pltpu.SemaphoreType.DMA((STEPS, 4)),
    ]
    field = jax.ShapeDtypeStruct((radial, *block), F32)
    wall = jax.ShapeDtypeStruct(wall_free.shape, F32)
    square = jax.ShapeDtypeStruct((128, 128), F32)
    drug, axial, substep, bound, wide, on_wide, off_wide = pl.pallas_call(
        kernel,
        out_shape=(
            field, field, wall, wall, jax.ShapeDtypeStruct((128, 384), BF16), square, square,
        ),
        in_specs=[hbm] * 9,
        out_specs=(vmem,) * 7,
        scratch_shapes=scratch,
        compiler_params=pltpu.CompilerParams(
            collective_id=0, has_side_effects=True, vmem_limit_bytes=40 * 2**20
        ),
    )(
        *(
            pltpu.with_memory_space_constraint(x, pltpu.HBM)
            for x in (
                populations, wall_free, wall_bound, wall_propagator,
                bind_on.reshape(1, 128), bind_off.reshape(1, 128),
                iface_sector.reshape(block), iface_line.reshape(block), strut_mask.reshape(block),
            )
        )
    )
    return pl.pallas_call(
        finish,
        out_shape=(field, field, wall, wall),
        in_specs=[vmem] * 7,
        out_specs=(hbm,) * 4,
        scratch_shapes=[
            wall_block,
            wall_block,
            pltpu.SemaphoreType.DMA((2 + 2 * (wall_free.shape[1] // WIDTH),)),
        ],
        compiler_params=pltpu.CompilerParams(vmem_limit_bytes=16 * 2**20),
    )(substep, bound, wide, on_wide, off_wide, drug, axial)


def solution(mesh):
    cells = P(None, "th", "ax")
    lines = P(None, ("ax", "th"))
    return jax.shard_map(
        per_device,
        mesh=mesh,
        in_specs=(
            P(None, None, "th", "ax"), lines, lines, P(), P(), P(),
            P(("ax", "th"), None), P(("ax", "th")), P(("ax", "th")),
        ),
        out_specs=(cells, cells, lines, lines),
        check_vma=False,
    )
```

```python
import functools

import jax
import jax.numpy as jnp
from jax import lax
from jax.experimental import pallas as pl
from jax.experimental.pallas import tpu as pltpu
from jax.sharding import PartitionSpec as P

STEPS = 4
RELAX_FLOW = 1.25
RELAX_DRUG = 1.1
PUSH_AXIAL = 0.0001
PERMEABILITY = 0.3
RELEASE_RATE = 0.5

VELOCITIES = [
    (0, 0, 0), (1, 0, 0), (-1, 0, 0), (0, 1, 0), (0, -1, 0), (0, 0, 1), (0, 0, -1),
    (1, 1, 0), (-1, -1, 0), (1, -1, 0), (-1, 1, 0), (1, 0, 1), (-1, 0, -1),
    (1, 0, -1), (-1, 0, 1), (0, 1, 1), (0, -1, -1), (0, 1, -1), (0, -1, 1),
    (0, 0, 0), (1, 0, 0), (-1, 0, 0), (0, 1, 0), (0, -1, 0), (0, 0, 1), (0, 0, -1),
]
OPPOSITE = [0, 2, 1, 4, 3, 6, 5, 8, 7, 10, 9, 12, 11, 14, 13, 16, 15, 18, 17, 19, 21, 20, 23, 22, 25, 24]
MIRROR = [0, 1, 2, 3, 4, 6, 5, 7, 8, 9, 10, 13, 14, 11, 12, 17, 18, 15, 16, 19, 20, 21, 22, 23, 25, 24]

S_UP = [3, 7, 10, 15, 17, 22]
S_DOWN = [4, 8, 9, 16, 18, 23]
MOVING = S_UP + S_DOWN
STILL = [q for q in range(26) if q not in MOVING]
Z_UP = [1, 7, 9, 11, 13, 20]
Z_DOWN = [2, 8, 10, 12, 14, 21]

F32 = jnp.float32
BF16 = jnp.bfloat16
MESH = pl.DeviceIdType.MESH


WIDTH = 256


def diffuse(wide, x):
    x_hi = x.astype(BF16)
    x_lo = (x - x_hi.astype(F32)).astype(BF16)
    return jnp.dot(
        wide[...], jnp.concatenate([x_hi, x_hi, x_lo], axis=0), preferred_element_type=F32
    )


def react(x, b, on, off):
    rate = on * x * (1.0 - b) - off * b
    return x - rate, b + rate


def wait_bytes(ref, sem):
    pltpu.make_async_copy(ref, ref, sem).wait()


def kernel(
    pops_hbm, free_hbm, bound_hbm, prop_hbm, on_hbm, off_hbm, sector_hbm, line_hbm, strut_hbm,
    drug_out, axial_out, substep, bound, wide, on_wide, off_wide,
    pops, free_in, prop, on_row, off_row, sector, line, strut, first_drug, first_free, load_sems,
    moving, still, drug_top, drug_now, speed_top, packed, faces, incoming, tops,
    onehot_hi, onehot_lo, lanes_lo, code_in, open_row, line_open, line_count, line_strut,
    table, sums, first_out, first_in, source,
    from_source, to_surface, propagated,
    table_send, table_recv, sums_send, sums_recv, first_send, first_recv,
    flow_send, flow_recv, top_send, top_recv,
):
    n_ax, n_th = lax.axis_size("ax"), lax.axis_size("th")
    ax, th = lax.axis_index("ax"), lax.axis_index("th")
    radial = pops.shape[1]
    top = radial - 1
    lane = lax.broadcasted_iota(jnp.int32, (8, 128), 1)
    ax_up, ax_down = lax.rem(ax + 1, n_ax), lax.rem(ax + n_ax - 1, n_ax)
    th_up, th_down = lax.rem(th + 1, n_th), lax.rem(th + n_th - 1, n_th)

    def peer(offset):
        return (ax, lax.rem(th + offset, n_th))

    beside = [
        (ax_up, th), (ax_down, th),
        (ax_up, th_up), (ax_up, th_down), (ax_down, th_up), (ax_down, th_down),
    ]
    barrier = pltpu.get_barrier_semaphore()
    greeted = [peer(o) for o in range(1, n_th)] + beside
    for device in greeted:
        pl.semaphore_signal(barrier, inc=1, device_id=device, device_id_type=MESH)

    loads = [
        (sector_hbm, sector), (line_hbm, line), (strut_hbm, strut),
        (pops_hbm.at[19:26, top], first_drug), (free_hbm.at[0:8, :], first_free),
        (prop_hbm, prop), (on_hbm, on_row), (off_hbm, off_row),
        (free_hbm, free_in), (pops_hbm, pops), (bound_hbm, bound),
    ]
    loads = [
        pltpu.make_async_copy(src, dst, load_sems.at[i]) for i, (src, dst) in enumerate(loads)
    ]
    for load in loads:
        load.start()
    for load in loads[:3]:
        load.wait()

    relative = lax.rem(sector[...] - th + n_th, n_th)
    line_all = line[...]
    line_lo = jnp.bitwise_and(line_all, 127)
    line_hi = jnp.right_shift(line_all, 7)
    code_out = relative * 8 + line_hi
    lanes_lo[...] = line_lo
    code_in[...] = lax.rem(n_th - relative, n_th) * 8 + line_hi
    n_blocks = 8 * n_th
    down_blocks = lax.broadcasted_iota(jnp.int32, (n_blocks, 128), 0)
    down_lanes = lax.broadcasted_iota(jnp.int32, (128, 128), 0)
    for s in range(8):
        part = pl.ds(128 * s, 128)
        onehot_hi[:, part] = jnp.where(down_blocks == code_out[s : s + 1, :], 1.0, 0.0).astype(BF16)
        onehot_lo[:, part] = jnp.where(down_lanes == line_lo[s : s + 1, :], 1.0, 0.0).astype(BF16)

    def by_line(values):
        high = values.astype(BF16).astype(F32)
        low = values - high
        total = None
        for s in range(0, 8, 2):
            part = pl.ds(128 * s, 256)
            ones = onehot_hi[:, part]
            rows = []
            for piece in (high, low):
                row = jnp.concatenate([piece[s : s + 1, :], piece[s + 1 : s + 2, :]], axis=1)
                rows.append(ones * row.astype(BF16))
            term = lax.dot_general(
                jnp.concatenate(rows, axis=0),
                onehot_lo[:, part],
                (((1,), (1,)), ((), ())),
                preferred_element_type=F32,
            )
            total = term if total is None else total + term
        return total[:n_blocks] + total[n_blocks:]

    def gathered(block):
        result = jnp.zeros((8, 128), F32)
        where = lanes_lo[...]
        code = code_in[...]
        for o in range(n_th):
            for hi in range(8):
                row = jnp.broadcast_to(block(o, hi), (8, 128))
                found = jnp.take_along_axis(row, where, axis=1, mode="promise_in_bounds")
                result = jnp.where(code == o * 8 + hi, found, result)
        return result

    def table_at(t, o):
        if t > 0:
            return table.at[t, o]
        return first_in.at[o, 2] if o else first_out.at[0, 2]

    def sums_at(t, o):
        if t > 0:
            return sums.at[1 if o else 0, t, o]
        return first_in.at[o, 3] if o else first_out.at[0, 3]

    def table_copy(t, o):
        return pltpu.make_async_remote_copy(
            table.at[t, 0], table.at[t, o], table_send.at[t], table_recv.at[t], peer(o), MESH
        )

    def sums_copy(t, o):
        return pltpu.make_async_remote_copy(
            sums.at[0, t, o], sums.at[1, t, o], sums_send.at[t], sums_recv.at[t], peer(o), MESH
        )

    def first_copy(o):
        return pltpu.make_async_remote_copy(
            first_out.at[o], first_in.at[o], first_send, first_recv, peer(o), MESH
        )

    def send_sums(t, surface):
        found = by_line(surface)
        for o in range(n_th):
            sums[0, t, o] = found[8 * o : 8 * o + 8]
        for o in range(1, n_th):
            sums_copy(t, o).start()

    for load in loads[3:5]:
        load.wait()
    strut_own = strut[...].astype(F32)
    surface = first_drug[0]
    for q in range(20, 26):
        surface = surface + first_drug[q - 19]
    found = by_line(surface)
    counts = by_line(jnp.ones((8, 128), F32))
    for o in range(n_th):
        first_out[o, 0] = strut_own
        first_out[o, 1] = counts[8 * o : 8 * o + 8]
        for c in range(8):
            first_out[o, 2, c : c + 1, :] = first_free[0:1, 128 * c : 128 * c + 128]
        first_out[o, 3] = found[8 * o : 8 * o + 8]
    pl.semaphore_wait(barrier, len(greeted))
    for o in range(1, n_th):
        first_copy(o).start()
    for q in range(19, 26):
        drug_now[q - 19] = first_drug[q - 19]
    drug_now[7] = surface

    for load in loads[5:]:
        load.wait()
    prop_all = prop[...]
    prop_hi = prop_all.astype(BF16)
    prop_lo = (prop_all - prop_hi.astype(F32)).astype(BF16)
    wide[...] = jnp.concatenate([prop_hi, prop_lo, prop_hi], axis=1)
    from_source[...] = jnp.broadcast_to(prop_all[:, 0:1], (128, 128))
    to_surface[...] = jnp.transpose(jnp.broadcast_to(prop_all[0:1, :], (128, 128)))
    on_wide[...] = jnp.transpose(jnp.broadcast_to(on_row[...], (128, 128)))
    off_wide[...] = jnp.transpose(jnp.broadcast_to(off_row[...], (128, 128)))
    n_lines = free_in.shape[1]
    for c in range(0, n_lines, WIDTH):
        propagated[:, c : c + WIDTH] = diffuse(wide, free_in[:, c : c + WIDTH])

    def own(p, q, r):
        if q in S_UP:
            return moving.at[p, MOVING.index(q), r, 8:16, :]
        if q in S_DOWN:
            return moving.at[p, MOVING.index(q), r, 0:8, :]
        return still.at[p, STILL.index(q), r]

    def shifted_s(p, q, r):
        if q in S_UP:
            return moving[p, MOVING.index(q), r, 7:15, :]
        if q in S_DOWN:
            return moving[p, MOVING.index(q), r, 1:9, :]
        return still[p, STILL.index(q), r]

    def spread_faces(t):
        for side, members in enumerate((Z_UP, Z_DOWN)):
            for k, q in enumerate(members):
                first = 8 - VELOCITIES[q][1]
                face = faces[t, side, first : first + 8, :]
                incoming[6 * side + k] = pltpu.roll(face, (128 - 16 * k) % 128, 1)

    def pack_faces(t, p):
        for side, members in enumerate((Z_UP, Z_DOWN)):
            block = jnp.zeros((8, 128), F32)
            for k, q in enumerate(members):
                face = jnp.zeros((8, 128), F32)
                for r in range(top + 1 if q < 19 else top):
                    face = jnp.where(lane == r + 1, own(p, q, r)[...], face)
                block = block + pltpu.roll(face, 16 * k, 1)
            packed[t, side] = block

    def pulled(p, q, r):
        value = shifted_s(p, q, r)
        if q in Z_UP:
            value = jnp.where(lane == r + 1, incoming[Z_UP.index(q)], value)
            return pltpu.roll(value, 127 - r, 1)
        if q in Z_DOWN:
            value = jnp.where(lane == r + 1, incoming[6 + Z_DOWN.index(q)], value)
            return pltpu.roll(value, 126 - r, 1)
        return value

    def own_plain(p, q, r):
        if q in Z_UP:
            return pltpu.roll(own(p, q, r)[...], 126 - r, 1)
        if q in Z_DOWN:
            return pltpu.roll(own(p, q, r)[...], 127 - r, 1)
        return own(p, q, r)[...]

    def moved(p, q, r, where):
        step_r = VELOCITIES[q][2]
        if step_r == 1 and where == "bottom":
            return pulled(p, MIRROR[q], r)
        if step_r == -1 and where == "top":
            return own_plain(p, OPPOSITE[q], r)
        return pulled(p, q, r - step_r)

    def collide_flow(f):
        d = {q: f[q] - f[q + 1] for q in (1, 3, 5, 7, 9, 11, 13, 15, 17)}
        density = f[0]
        for q in range(1, 19):
            density = density + f[q]
        jz = d[1] + d[7] + d[9] + d[11] + d[13] + PUSH_AXIAL
        js = d[3] + d[7] - d[9] + d[15] + d[17]
        jr = d[5] + d[11] - d[13] + d[15] - d[17]
        uz, us, ur = jz / density, js / density, jr / density
        base = 1.0 - 1.5 * (uz * uz + us * us + ur * ur)
        edge = density * (RELAX_FLOW / 36.0)
        face = density * (RELAX_FLOW / 18.0)
        keep = 1.0 - RELAX_FLOW
        post = {0: keep * f[0] + density * (RELAX_FLOW / 3.0) * base}
        along = {
            1: uz, 3: us, 5: ur, 7: uz + us, 9: uz - us,
            11: uz + ur, 13: uz - ur, 15: us + ur, 17: us - ur,
        }
        for q, speed in along.items():
            weight = face if q < 7 else edge
            even = weight * (base + 4.5 * speed * speed)
            odd = weight * (3.0 * speed)
            post[q] = keep * f[q] + (even + odd)
            post[q + 1] = keep * f[q + 1] + (even - odd)
        return post, (uz, us, ur)

    def collide_drug(f, total, speeds):
        keep = 1.0 - RELAX_DRUG
        share = total * (RELAX_DRUG * 0.125)
        post = {19: keep * f[19] + 2.0 * share}
        for q, speed in zip((20, 22, 24), speeds):
            odd = 4.0 * speed
            post[q] = keep * f[q] + share * (1.0 + odd)
            post[q + 1] = keep * f[q + 1] + share * (1.0 - odd)
        return post

    def layers(read, p, rows):
        loaded = []
        for r, where in rows:
            members = range(19 if where == "top" else 26)
            loaded.append({q: read(q, r, where) for q in members})
        posts = []
        for (_, where), f in zip(rows, loaded):
            post, speeds = collide_flow(f)
            if where == "top":
                for i in range(3):
                    speed_top[i] = speeds[i]
            else:
                total = f[19]
                for q in range(20, 26):
                    total = total + f[q]
                post.update(collide_drug(f, total, speeds))
            posts.append(post)
        for (r, _), post in zip(rows, posts):
            for q, value in post.items():
                if q in Z_UP:
                    value = pltpu.roll(value, r + 2, 1)
                elif q in Z_DOWN:
                    value = pltpu.roll(value, r + 1, 1)
                own(p, q, r)[...] = value

    def flow_copies(t, p):
        def copy(src, dst, device, i):
            return pltpu.make_async_remote_copy(
                src, dst, flow_send.at[t, i], flow_recv.at[t, i], device, MESH
            )

        up, down = (ax, th_up), (ax, th_down)
        copies = [
            copy(moving.at[p, 0:5, :, 15, :], moving.at[p, 0:5, :, 7, :], up, 0),
            copy(moving.at[p, 6:11, :, 0, :], moving.at[p, 6:11, :, 8, :], down, 1),
            copy(moving.at[p, 5, 0:top, 15, :], moving.at[p, 5, 0:top, 7, :], up, 2),
            copy(moving.at[p, 11, 0:top, 0, :], moving.at[p, 11, 0:top, 8, :], down, 3),
        ]
        for side, to in ((0, ax_up), (1, ax_down)):
            i = 4 + 3 * side
            copies += [
                copy(packed.at[t, side], faces.at[t, side, 8:16, :], (to, th), i),
                copy(packed.at[t, side, 7:8, :], faces.at[t, side, 7:8, :], (to, th_up), i + 1),
                copy(packed.at[t, side, 0:1, :], faces.at[t, side, 16:17, :], (to, th_down), i + 2),
            ]
        return copies

    def collide_all(t, p):
        if t == 0:
            read = lambda q, r, where: pops[q, r]
        else:
            spread_faces(t - 1)
            read = functools.partial(moved, 1 - p)
        layers(read, p, [(0, "bottom"), (top, "top")])

        def pair(i, carry):
            layers(read, p, [(2 * i + 1, "middle"), (2 * i + 2, "middle")])
            return carry

        lax.fori_loop(0, (top - 1) // 2, pair, 0)
        pack_faces(t, p)
        for copy in flow_copies(t, p):
            copy.start()

    def top_copies(t, p):
        def copy(src, dst, device, i):
            return pltpu.make_async_remote_copy(
                src, dst, top_send.at[t, i], top_recv.at[t, i], device, MESH
            )

        return [
            copy(drug_top.at[p, 1, 0:8, :], tops.at[t, 0], (ax_up, th), 0),
            copy(drug_top.at[p, 2, 0:8, :], tops.at[t, 1], (ax_down, th), 1),
            copy(drug_top.at[p, 3, 15, :], drug_top.at[p, 3, 7, :], (ax, th_up), 2),
            copy(drug_top.at[p, 4, 0, :], drug_top.at[p, 4, 8, :], (ax, th_down), 3),
        ]

    def wall_flux(t, p):
        if t > 0:
            wait_bytes(table.at[t, pl.ds(1, n_th - 1)], table_recv.at[t])
        free_rows = gathered(lambda o, hi: table_at(t, o)[hi : hi + 1, :])
        surface = drug_now[7]
        flux = open_row[...] * (surface - free_rows)
        lowered = {19: drug_now[0] - 0.25 * flux}
        for q in range(20, 26):
            lowered[q] = drug_now[q - 19] - 0.125 * flux
        post = collide_drug(lowered, surface - flux, [speed_top[i] for i in range(3)])
        drug_top[p, 1, 0:8, :] = post[20]
        drug_top[p, 2, 0:8, :] = post[21]
        drug_top[p, 3, 8:16, :] = post[22]
        drug_top[p, 4, 0:8, :] = post[23]
        for copy in top_copies(t, p):
            copy.start()
        drug_top[p, 0, 0:8, :] = post[19]
        drug_top[p, 5, 0:8, :] = post[24]
        own(p, 25, top)[...] = post[25]

    def wall_first(t, send):
        if t > 0:
            wait_bytes(sums.at[1, t, pl.ds(1, n_th - 1)], sums_recv.at[t])
        total = sums_at(t, 0)[...]
        for o in range(1, n_th):
            total = total + sums_at(t, o)[...]
        flux = line_open[...] * (total - line_count[...] * table_at(t, 0)[...])
        source[...] = flux + RELEASE_RATE * line_strut[...]
        for c in range(8):
            part = pl.ds(128 * c, 128)
            x = propagated[:, part] + from_source[...] * source[c : c + 1, :]
            x, b = react(x, bound[:, part], on_wide[...], off_wide[...])
            substep[:, part] = x
            bound[:, part] = b
            if send:
                x = jnp.sum(to_surface[...] * x, axis=0, keepdims=True)
                x, _ = react(x, b[0:1, :], on_wide[0:1, :], off_wide[0:1, :])
                table[t + 1, 0, c : c + 1, :] = x
        if send:
            for o in range(1, n_th):
                table_copy(t + 1, o).start()

    def wall_second():
        wide_on = jnp.concatenate([on_wide[...]] * (WIDTH // 128), axis=1)
        wide_off = jnp.concatenate([off_wide[...]] * (WIDTH // 128), axis=1)
        for c in range(0, n_lines, WIDTH):
            part = pl.ds(c, WIDTH)
            x, b = react(diffuse(wide, substep[:, part]), bound[:, part], wide_on, wide_off)
            bound[:, part] = b
            propagated[:, part] = diffuse(wide, x)

    def top_moved(t, p):
        f = {19: drug_top[p, 0, 0:8, :]}
        f[20] = jnp.where(lane == 0, pltpu.roll(tops[t, 0], 1, 1), pltpu.roll(drug_top[p, 1, 0:8, :], 1, 1))
        f[21] = jnp.where(lane == 127, pltpu.roll(tops[t, 1], 127, 1), pltpu.roll(drug_top[p, 2, 0:8, :], 127, 1))
        f[22] = drug_top[p, 3, 7:15, :]
        f[23] = drug_top[p, 4, 1:9, :]
        f[24] = own(p, 24, top - 1)[...]
        f[25] = drug_top[p, 5, 0:8, :]
        total = f[19]
        for q in range(20, 26):
            total = total + f[q]
        return f, total

    def wait_tops(t, p):
        for copy in top_copies(t, p):
            copy.wait()

    def wait_flow(t, p):
        for copy in flow_copies(t, p):
            copy.wait()

    def wait_coupling_sends(t):
        if t == 0:
            wait_bytes(first_in.at[pl.ds(1, n_th - 1)], first_send)
            return
        wait_bytes(table.at[t, pl.ds(1, n_th - 1)], table_send.at[t])
        wait_bytes(sums.at[1, t, pl.ds(1, n_th - 1)], sums_send.at[t])

    collide_all(0, 0)
    wait_bytes(first_in.at[pl.ds(1, n_th - 1)], first_recv)
    line_strut[...] = strut_own
    line_open[...] = PERMEABILITY * (1.0 - strut_own)
    count = first_out[0, 1]
    for o in range(1, n_th):
        count = count + first_in[o, 1]
    line_count[...] = count
    covered = gathered(lambda o, hi: (first_in if o else first_out)[o, 0, hi : hi + 1, :])
    open_row[...] = PERMEABILITY * (1.0 - covered)

    def wall_side(t, p):
        wait_tops(t, p)
        f, total = top_moved(t, p)
        for q in range(19, 26):
            drug_now[q - 19] = f[q]
        drug_now[7] = total
        send_sums(t + 1, total)

    for t in range(STEPS - 1):
        p = t % 2
        wall_flux(t, p)
        wall_first(t, True)
        if p == 1:
            wall_side(t, p)
        wall_second()
        wait_coupling_sends(t)
        wait_flow(t, p)
        collide_all(t + 1, 1 - p)
        if p == 0:
            wall_side(t, p)

    t, p = STEPS - 1, (STEPS - 1) % 2
    wall_flux(t, p)
    wait_flow(t, p)

    def results(rows):
        for r, where in rows:
            flow = None
            for q in Z_UP[:5]:
                term = moved(p, q, r, where) - moved(p, OPPOSITE[q], r, where)
                flow = term if flow is None else flow + term
            axial_out[r] = flow
            if where != "top":
                total = moved(p, 19, r, where)
                for q in range(20, 26):
                    total = total + moved(p, q, r, where)
                drug_out[r] = total

    def results_pair(i, carry):
        results([(2 * i + 1, "middle"), (2 * i + 2, "middle")])
        return carry

    spread_faces(t)
    results([(0, "bottom"), (top, "top")])
    lax.fori_loop(0, (top - 1) // 2, results_pair, 0)
    wall_first(t, False)
    wait_coupling_sends(t)
    wait_tops(t, p)
    drug_out[top] = top_moved(t, p)[1]


def finish(
    substep, bound_in, wide, on_wide, off_wide, drug_in, axial_in,
    drug, axial, free, bound,
    free_part, bound_part, sems,
):
    copies = [
        pltpu.make_async_copy(drug_in, drug, sems.at[0]),
        pltpu.make_async_copy(axial_in, axial, sems.at[1]),
    ]
    for copy in copies:
        copy.start()
    wide_on = jnp.concatenate([on_wide[...]] * (WIDTH // 128), axis=1)
    wide_off = jnp.concatenate([off_wide[...]] * (WIDTH // 128), axis=1)
    for i in range(substep.shape[1] // WIDTH):
        part = pl.ds(i * WIDTH, WIDTH)
        x, b = react(diffuse(wide, substep[:, part]), bound_in[:, part], wide_on, wide_off)
        free_part[:, part] = x
        bound_part[:, part] = b
        for k, (src, dst) in enumerate(((free_part, free), (bound_part, bound))):
            copy = pltpu.make_async_copy(src.at[:, part], dst.at[:, part], sems.at[2 + 2 * i + k])
            copy.start()
            copies.append(copy)
    for copy in copies:
        copy.wait()


def per_device(
    populations, wall_free, wall_bound, wall_propagator, bind_on, bind_off,
    iface_sector, iface_line, strut_mask,
):
    n_th = lax.axis_size("th")
    radial = populations.shape[1]
    vmem = pl.BlockSpec(memory_space=pltpu.VMEM)
    hbm = pl.BlockSpec(memory_space=pltpu.HBM)
    block = (8, 128)
    wall_block = pltpu.VMEM(wall_free.shape, F32)
    scratch = [
        pltpu.VMEM(populations.shape, F32),
        wall_block,
        pltpu.VMEM((128, 128), F32),
        pltpu.VMEM((1, 128), F32),
        pltpu.VMEM((1, 128), F32),
        pltpu.VMEM(block, jnp.int32),
        pltpu.VMEM(block, jnp.int32),
        pltpu.VMEM(block, jnp.int32),
        pltpu.VMEM((7, *block), F32),
        pltpu.VMEM((8, wall_free.shape[1]), F32),
        pltpu.SemaphoreType.DMA((11,)),
        pltpu.VMEM((2, len(MOVING), radial, 16, 128), F32),
        pltpu.VMEM((2, len(STILL), radial, 8, 128), F32),
        pltpu.VMEM((2, 6, 16, 128), F32),
        pltpu.VMEM((8, *block), F32),
        pltpu.VMEM((3, *block), F32),
        pltpu.VMEM((STEPS, 2, *block), F32),
        pltpu.VMEM((STEPS, 2, 24, 128), F32),
        pltpu.VMEM((12, *block), F32),
        pltpu.VMEM((STEPS, 2, *block), F32),
        pltpu.VMEM((8 * n_th, 1024), BF16),
        pltpu.VMEM((128, 1024), BF16),
        pltpu.VMEM(block, jnp.int32),
        pltpu.VMEM(block, jnp.int32),
        pltpu.VMEM(block, F32),
        pltpu.VMEM(block, F32),
        pltpu.VMEM(block, F32),
        pltpu.VMEM(block, F32),
        pltpu.VMEM((STEPS, n_th, *block), F32),
        pltpu.VMEM((2, STEPS, n_th, *block), F32),
        pltpu.VMEM((n_th, 4, *block), F32),
        pltpu.VMEM((n_th, 4, *block), F32),
        pltpu.VMEM(block, F32),
        pltpu.VMEM((128, 128), F32),
        pltpu.VMEM((128, 128), F32),
        wall_block,
        pltpu.SemaphoreType.DMA((STEPS,)),
        pltpu.SemaphoreType.DMA((STEPS,)),
        pltpu.SemaphoreType.DMA((STEPS,)),
        pltpu.SemaphoreType.DMA((STEPS,)),
        pltpu.SemaphoreType.DMA,
        pltpu.SemaphoreType.DMA,
        pltpu.SemaphoreType.DMA((STEPS, 10)),
        pltpu.SemaphoreType.DMA((STEPS, 10)),
        pltpu.SemaphoreType.DMA((STEPS, 4)),
        pltpu.SemaphoreType.DMA((STEPS, 4)),
    ]
    field = jax.ShapeDtypeStruct((radial, *block), F32)
    wall = jax.ShapeDtypeStruct(wall_free.shape, F32)
    square = jax.ShapeDtypeStruct((128, 128), F32)
    drug, axial, substep, bound, wide, on_wide, off_wide = pl.pallas_call(
        kernel,
        out_shape=(
            field, field, wall, wall, jax.ShapeDtypeStruct((128, 384), BF16), square, square,
        ),
        in_specs=[hbm] * 9,
        out_specs=(vmem,) * 7,
        scratch_shapes=scratch,
        compiler_params=pltpu.CompilerParams(
            collective_id=0, has_side_effects=True, vmem_limit_bytes=40 * 2**20
        ),
    )(
        *(
            pltpu.with_memory_space_constraint(x, pltpu.HBM)
            for x in (
                populations, wall_free, wall_bound, wall_propagator,
                bind_on.reshape(1, 128), bind_off.reshape(1, 128),
                iface_sector.reshape(block), iface_line.reshape(block), strut_mask.reshape(block),
            )
        )
    )
    return pl.pallas_call(
        finish,
        out_shape=(field, field, wall, wall),
        in_specs=[vmem] * 7,
        out_specs=(hbm,) * 4,
        scratch_shapes=[
            wall_block,
            wall_block,
            pltpu.SemaphoreType.DMA((2 + 2 * (wall_free.shape[1] // WIDTH),)),
        ],
        compiler_params=pltpu.CompilerParams(vmem_limit_bytes=16 * 2**20),
    )(substep, bound, wide, on_wide, off_wide, drug, axial)


def solution(mesh):
    cells = P(None, "th", "ax")
    lines = P(None, ("ax", "th"))
    return jax.shard_map(
        per_device,
        mesh=mesh,
        in_specs=(
            P(None, None, "th", "ax"), lines, lines, P(), P(), P(),
            P(("ax", "th"), None), P(("ax", "th")), P(("ax", "th")),
        ),
        out_specs=(cells, cells, lines, lines),
        check_vma=False,
    )
```

```python
import functools

import jax
import jax.numpy as jnp
from jax import lax
from jax.experimental import pallas as pl
from jax.experimental.pallas import tpu as pltpu
from jax.sharding import PartitionSpec as P

STEPS = 4
RELAX_FLOW = 1.25
RELAX_DRUG = 1.1
PUSH_AXIAL = 0.0001
PERMEABILITY = 0.3
RELEASE_RATE = 0.5

VELOCITIES = [
    (0, 0, 0), (1, 0, 0), (-1, 0, 0), (0, 1, 0), (0, -1, 0), (0, 0, 1), (0, 0, -1),
    (1, 1, 0), (-1, -1, 0), (1, -1, 0), (-1, 1, 0), (1, 0, 1), (-1, 0, -1),
    (1, 0, -1), (-1, 0, 1), (0, 1, 1), (0, -1, -1), (0, 1, -1), (0, -1, 1),
    (0, 0, 0), (1, 0, 0), (-1, 0, 0), (0, 1, 0), (0, -1, 0), (0, 0, 1), (0, 0, -1),
]
OPPOSITE = [0, 2, 1, 4, 3, 6, 5, 8, 7, 10, 9, 12, 11, 14, 13, 16, 15, 18, 17, 19, 21, 20, 23, 22, 25, 24]
MIRROR = [0, 1, 2, 3, 4, 6, 5, 7, 8, 9, 10, 13, 14, 11, 12, 17, 18, 15, 16, 19, 20, 21, 22, 23, 25, 24]

S_UP = [3, 7, 10, 15, 17, 22]
S_DOWN = [4, 8, 9, 16, 18, 23]
MOVING = S_UP + S_DOWN
STILL = [q for q in range(26) if q not in MOVING]
Z_UP = [1, 7, 9, 11, 13, 20]
Z_DOWN = [2, 8, 10, 12, 14, 21]

F32 = jnp.float32
BF16 = jnp.bfloat16
MESH = pl.DeviceIdType.MESH


WIDTH = 256


def diffuse(wide, x):
    x_hi = x.astype(BF16)
    x_lo = (x - x_hi.astype(F32)).astype(BF16)
    return jnp.dot(
        wide[...], jnp.concatenate([x_hi, x_hi, x_lo], axis=0), preferred_element_type=F32
    )


def react(x, b, on, off):
    rate = on * x * (1.0 - b) - off * b
    return x - rate, b + rate


def wait_bytes(ref, sem):
    pltpu.make_async_copy(ref, ref, sem).wait()


def kernel(
    pops_hbm, free_hbm, bound_hbm, prop_hbm, on_hbm, off_hbm, sector_hbm, line_hbm, strut_hbm,
    drug_out, axial_out, substep, bound, wide, on_wide, off_wide,
    pops, free_in, prop, on_row, off_row, sector, line, strut, first_drug, first_free, load_sems,
    moving, still, drug_top, drug_now, speed_top, packed, faces, incoming, tops,
    onehot_hi, onehot_lo, lanes_lo, code_in, open_row, line_open, line_count, line_strut,
    table, sums, first_out, first_in, source,
    from_source, to_surface, propagated,
    table_send, table_recv, sums_send, sums_recv, first_send, first_recv,
    edge_send, edge_recv, flow_send, flow_recv, top_send, top_recv,
):
    n_ax, n_th = lax.axis_size("ax"), lax.axis_size("th")
    ax, th = lax.axis_index("ax"), lax.axis_index("th")
    radial = pops.shape[1]
    top = radial - 1
    lane = lax.broadcasted_iota(jnp.int32, (8, 128), 1)
    ax_up, ax_down = lax.rem(ax + 1, n_ax), lax.rem(ax + n_ax - 1, n_ax)
    th_up, th_down = lax.rem(th + 1, n_th), lax.rem(th + n_th - 1, n_th)

    def peer(offset):
        return (ax, lax.rem(th + offset, n_th))

    beside = [
        (ax_up, th), (ax_down, th),
        (ax_up, th_up), (ax_up, th_down), (ax_down, th_up), (ax_down, th_down),
    ]
    barrier = pltpu.get_barrier_semaphore()
    greeted = [peer(o) for o in range(1, n_th)] + beside
    for device in greeted:
        pl.semaphore_signal(barrier, inc=1, device_id=device, device_id_type=MESH)

    loads = [
        (sector_hbm, sector), (line_hbm, line), (strut_hbm, strut),
        (pops_hbm.at[19:26, top], first_drug), (free_hbm.at[0:8, :], first_free),
        (prop_hbm, prop), (on_hbm, on_row), (off_hbm, off_row),
        (free_hbm, free_in), (pops_hbm, pops), (bound_hbm, bound),
    ]
    loads = [
        pltpu.make_async_copy(src, dst, load_sems.at[i]) for i, (src, dst) in enumerate(loads)
    ]
    for load in loads:
        load.start()
    for load in loads[:3]:
        load.wait()

    relative = lax.rem(sector[...] - th + n_th, n_th)
    line_all = line[...]
    line_lo = jnp.bitwise_and(line_all, 127)
    line_hi = jnp.right_shift(line_all, 7)
    code_out = relative * 8 + line_hi
    lanes_lo[...] = line_lo
    code_in[...] = lax.rem(n_th - relative, n_th) * 8 + line_hi
    n_blocks = 8 * n_th
    down_blocks = lax.broadcasted_iota(jnp.int32, (n_blocks, 128), 0)
    down_lanes = lax.broadcasted_iota(jnp.int32, (128, 128), 0)
    for s in range(8):
        part = pl.ds(128 * s, 128)
        onehot_hi[:, part] = jnp.where(down_blocks == code_out[s : s + 1, :], 1.0, 0.0).astype(BF16)
        onehot_lo[:, part] = jnp.where(down_lanes == line_lo[s : s + 1, :], 1.0, 0.0).astype(BF16)

    def by_line(values):
        high = values.astype(BF16).astype(F32)
        low = values - high
        total = None
        for s in range(0, 8, 2):
            part = pl.ds(128 * s, 256)
            ones = onehot_hi[:, part]
            rows = []
            for piece in (high, low):
                row = jnp.concatenate([piece[s : s + 1, :], piece[s + 1 : s + 2, :]], axis=1)
                rows.append(ones * row.astype(BF16))
            term = lax.dot_general(
                jnp.concatenate(rows, axis=0),
                onehot_lo[:, part],
                (((1,), (1,)), ((), ())),
                preferred_element_type=F32,
            )
            total = term if total is None else total + term
        return total[:n_blocks] + total[n_blocks:]

    def gathered(block):
        result = jnp.zeros((8, 128), F32)
        where = lanes_lo[...]
        code = code_in[...]
        for o in range(n_th):
            for hi in range(8):
                row = jnp.broadcast_to(block(o, hi), (8, 128))
                found = jnp.take_along_axis(row, where, axis=1, mode="promise_in_bounds")
                result = jnp.where(code == o * 8 + hi, found, result)
        return result

    def table_at(t, o):
        if t > 0:
            return table.at[t, o]
        return first_in.at[o, 2] if o else first_out.at[0, 2]

    def sums_at(t, o):
        if t > 0:
            return sums.at[1 if o else 0, t, o]
        return first_in.at[o, 3] if o else first_out.at[0, 3]

    def table_copy(t, o):
        return pltpu.make_async_remote_copy(
            table.at[t, 0], table.at[t, o], table_send.at[t], table_recv.at[t], peer(o), MESH
        )

    def sums_copy(t, o):
        return pltpu.make_async_remote_copy(
            sums.at[0, t, o], sums.at[1, t, o], sums_send.at[t], sums_recv.at[t], peer(o), MESH
        )

    def first_copy(o):
        return pltpu.make_async_remote_copy(
            first_out.at[o], first_in.at[o], first_send, first_recv, peer(o), MESH
        )

    def send_sums(t, surface):
        found = by_line(surface)
        for o in range(n_th):
            sums[0, t, o] = found[8 * o : 8 * o + 8]
        for o in range(1, n_th):
            sums_copy(t, o).start()

    for load in loads[3:5]:
        load.wait()
    strut_own = strut[...].astype(F32)
    surface = first_drug[0]
    for q in range(20, 26):
        surface = surface + first_drug[q - 19]
    found = by_line(surface)
    counts = by_line(jnp.ones((8, 128), F32))
    for o in range(n_th):
        first_out[o, 0] = strut_own
        first_out[o, 1] = counts[8 * o : 8 * o + 8]
        for c in range(8):
            first_out[o, 2, c : c + 1, :] = first_free[0:1, 128 * c : 128 * c + 128]
        first_out[o, 3] = found[8 * o : 8 * o + 8]
    pl.semaphore_wait(barrier, len(greeted))
    for o in range(1, n_th):
        first_copy(o).start()
    for q in range(19, 26):
        drug_now[q - 19] = first_drug[q - 19]
    drug_now[7] = surface

    for load in loads[5:]:
        load.wait()
    prop_all = prop[...]
    prop_hi = prop_all.astype(BF16)
    prop_lo = (prop_all - prop_hi.astype(F32)).astype(BF16)
    wide[...] = jnp.concatenate([prop_hi, prop_lo, prop_hi], axis=1)
    from_source[...] = jnp.broadcast_to(prop_all[:, 0:1], (128, 128))
    to_surface[...] = jnp.transpose(jnp.broadcast_to(prop_all[0:1, :], (128, 128)))
    on_wide[...] = jnp.transpose(jnp.broadcast_to(on_row[...], (128, 128)))
    off_wide[...] = jnp.transpose(jnp.broadcast_to(off_row[...], (128, 128)))
    n_lines = free_in.shape[1]
    for c in range(0, n_lines, WIDTH):
        propagated[:, c : c + WIDTH] = diffuse(wide, free_in[:, c : c + WIDTH])

    def own(p, q, r):
        if q in S_UP:
            return moving.at[p, MOVING.index(q), r, 8:16, :]
        if q in S_DOWN:
            return moving.at[p, MOVING.index(q), r, 0:8, :]
        return still.at[p, STILL.index(q), r]

    def shifted_s(p, q, r):
        if q in S_UP:
            return moving[p, MOVING.index(q), r, 7:15, :]
        if q in S_DOWN:
            return moving[p, MOVING.index(q), r, 1:9, :]
        return still[p, STILL.index(q), r]

    def spread_faces(t):
        for side, members in enumerate((Z_UP, Z_DOWN)):
            for k, q in enumerate(members):
                first = 8 - VELOCITIES[q][1]
                face = faces[t, side, first : first + 8, :]
                incoming[6 * side + k] = pltpu.roll(face, (128 - 16 * k) % 128, 1)

    def pack_faces(t, p):
        for side, members in enumerate((Z_UP, Z_DOWN)):
            block = jnp.zeros((8, 128), F32)
            for k, q in enumerate(members):
                face = jnp.zeros((8, 128), F32)
                for r in range(top + 1 if q < 19 else top):
                    face = jnp.where(lane == r + 1, own(p, q, r)[...], face)
                block = block + pltpu.roll(face, 16 * k, 1)
            packed[t, side] = block

    def pulled(p, q, r):
        value = shifted_s(p, q, r)
        if q in Z_UP:
            value = jnp.where(lane == r + 1, incoming[Z_UP.index(q)], value)
            return pltpu.roll(value, 127 - r, 1)
        if q in Z_DOWN:
            value = jnp.where(lane == r + 1, incoming[6 + Z_DOWN.index(q)], value)
            return pltpu.roll(value, 126 - r, 1)
        return value

    def own_plain(p, q, r):
        if q in Z_UP:
            return pltpu.roll(own(p, q, r)[...], 126 - r, 1)
        if q in Z_DOWN:
            return pltpu.roll(own(p, q, r)[...], 127 - r, 1)
        return own(p, q, r)[...]

    def moved(p, q, r, where):
        step_r = VELOCITIES[q][2]
        if step_r == 1 and where == "bottom":
            return pulled(p, MIRROR[q], r)
        if step_r == -1 and where == "top":
            return own_plain(p, OPPOSITE[q], r)
        return pulled(p, q, r - step_r)

    def collide_flow(f):
        d = {q: f[q] - f[q + 1] for q in (1, 3, 5, 7, 9, 11, 13, 15, 17)}
        density = f[0]
        for q in range(1, 19):
            density = density + f[q]
        jz = d[1] + d[7] + d[9] + d[11] + d[13] + PUSH_AXIAL
        js = d[3] + d[7] - d[9] + d[15] + d[17]
        jr = d[5] + d[11] - d[13] + d[15] - d[17]
        uz, us, ur = jz / density, js / density, jr / density
        base = 1.0 - 1.5 * (uz * uz + us * us + ur * ur)
        edge = density * (RELAX_FLOW / 36.0)
        face = density * (RELAX_FLOW / 18.0)
        keep = 1.0 - RELAX_FLOW
        post = {0: keep * f[0] + density * (RELAX_FLOW / 3.0) * base}
        along = {
            1: uz, 3: us, 5: ur, 7: uz + us, 9: uz - us,
            11: uz + ur, 13: uz - ur, 15: us + ur, 17: us - ur,
        }
        for q, speed in along.items():
            weight = face if q < 7 else edge
            even = weight * (base + 4.5 * speed * speed)
            odd = weight * (3.0 * speed)
            post[q] = keep * f[q] + (even + odd)
            post[q + 1] = keep * f[q + 1] + (even - odd)
        return post, (uz, us, ur)

    def collide_drug(f, total, speeds):
        keep = 1.0 - RELAX_DRUG
        share = total * (RELAX_DRUG * 0.125)
        post = {19: keep * f[19] + 2.0 * share}
        for q, speed in zip((20, 22, 24), speeds):
            odd = 4.0 * speed
            post[q] = keep * f[q] + share * (1.0 + odd)
            post[q + 1] = keep * f[q + 1] + share * (1.0 - odd)
        return post

    def layers(read, p, rows):
        loaded = []
        for r, where in rows:
            members = range(19 if where == "top" else 26)
            loaded.append({q: read(q, r, where) for q in members})
        posts = []
        for (_, where), f in zip(rows, loaded):
            post, speeds = collide_flow(f)
            if where == "top":
                for i in range(3):
                    speed_top[i] = speeds[i]
            else:
                total = f[19]
                for q in range(20, 26):
                    total = total + f[q]
                post.update(collide_drug(f, total, speeds))
            posts.append(post)
        for (r, _), post in zip(rows, posts):
            for q, value in post.items():
                if q in Z_UP:
                    value = pltpu.roll(value, r + 2, 1)
                elif q in Z_DOWN:
                    value = pltpu.roll(value, r + 1, 1)
                own(p, q, r)[...] = value

    def flow_copies(t, p):
        def copy(src, dst, device, i):
            return pltpu.make_async_remote_copy(
                src, dst, flow_send.at[t, i], flow_recv.at[t, i], device, MESH
            )

        copies = []
        for side, to in ((0, ax_up), (1, ax_down)):
            i = 3 * side
            copies += [
                copy(packed.at[t, side], faces.at[t, side, 8:16, :], (to, th), i),
                copy(packed.at[t, side, 7:8, :], faces.at[t, side, 7:8, :], (to, th_up), i + 1),
                copy(packed.at[t, side, 0:1, :], faces.at[t, side, 16:17, :], (to, th_down), i + 2),
            ]
        return copies

    def send_edges(t, p, r, count, members):
        rows = pl.ds(r, count)
        for side, first, src, dst, to in ((0, 0, 15, 7, th_up), (1, 6, 0, 8, th_down)):
            movers = pl.ds(first, members)
            pltpu.make_async_remote_copy(
                moving.at[p, movers, rows, src, :], moving.at[p, movers, rows, dst, :],
                edge_send.at[t, side], edge_recv.at[t, side], (ax, to), MESH,
            ).start()

    def wait_edges(t):
        all_rows = pops.at[0:19, 0:5, 0, :]
        assert 19 * 5 == 6 * top + 5
        for side in range(2):
            wait_bytes(all_rows, edge_send.at[t, side])
            wait_bytes(all_rows, edge_recv.at[t, side])

    def collide_all(t, p):
        if t == 0:
            read = lambda q, r, where: pops[q, r]
        else:
            spread_faces(t - 1)
            read = functools.partial(moved, 1 - p)
        layers(read, p, [(0, "bottom"), (top, "top")])
        send_edges(t, p, 0, 1, 6)
        send_edges(t, p, top, 1, 5)

        def pair(i, carry):
            layers(read, p, [(2 * i + 1, "middle"), (2 * i + 2, "middle")])
            send_edges(t, p, 2 * i + 1, 2, 6)
            return carry

        lax.fori_loop(0, (top - 1) // 2, pair, 0)
        pack_faces(t, p)
        for copy in flow_copies(t, p):
            copy.start()

    def top_copies(t, p):
        def copy(src, dst, device, i):
            return pltpu.make_async_remote_copy(
                src, dst, top_send.at[t, i], top_recv.at[t, i], device, MESH
            )

        return [
            copy(drug_top.at[p, 1, 0:8, :], tops.at[t, 0], (ax_up, th), 0),
            copy(drug_top.at[p, 2, 0:8, :], tops.at[t, 1], (ax_down, th), 1),
            copy(drug_top.at[p, 3, 15, :], drug_top.at[p, 3, 7, :], (ax, th_up), 2),
            copy(drug_top.at[p, 4, 0, :], drug_top.at[p, 4, 8, :], (ax, th_down), 3),
        ]

    def wall_flux(t, p):
        if t > 0:
            wait_bytes(table.at[t, pl.ds(1, n_th - 1)], table_recv.at[t])
        free_rows = gathered(lambda o, hi: table_at(t, o)[hi : hi + 1, :])
        surface = drug_now[7]
        flux = open_row[...] * (surface - free_rows)
        lowered = {19: drug_now[0] - 0.25 * flux}
        for q in range(20, 26):
            lowered[q] = drug_now[q - 19] - 0.125 * flux
        post = collide_drug(lowered, surface - flux, [speed_top[i] for i in range(3)])
        drug_top[p, 1, 0:8, :] = post[20]
        drug_top[p, 2, 0:8, :] = post[21]
        drug_top[p, 3, 8:16, :] = post[22]
        drug_top[p, 4, 0:8, :] = post[23]
        for copy in top_copies(t, p):
            copy.start()
        drug_top[p, 0, 0:8, :] = post[19]
        drug_top[p, 5, 0:8, :] = post[24]
        own(p, 25, top)[...] = post[25]

    def wall_first(t, send):
        if t > 0:
            wait_bytes(sums.at[1, t, pl.ds(1, n_th - 1)], sums_recv.at[t])
        total = sums_at(t, 0)[...]
        for o in range(1, n_th):
            total = total + sums_at(t, o)[...]
        flux = line_open[...] * (total - line_count[...] * table_at(t, 0)[...])
        source[...] = flux + RELEASE_RATE * line_strut[...]
        for c in range(8):
            part = pl.ds(128 * c, 128)
            x = propagated[:, part] + from_source[...] * source[c : c + 1, :]
            x, b = react(x, bound[:, part], on_wide[...], off_wide[...])
            substep[:, part] = x
            bound[:, part] = b
            if send:
                x = jnp.sum(to_surface[...] * x, axis=0, keepdims=True)
                x, _ = react(x, b[0:1, :], on_wide[0:1, :], off_wide[0:1, :])
                table[t + 1, 0, c : c + 1, :] = x
        if send:
            for o in range(1, n_th):
                table_copy(t + 1, o).start()

    def wall_second():
        wide_on = jnp.concatenate([on_wide[...]] * (WIDTH // 128), axis=1)
        wide_off = jnp.concatenate([off_wide[...]] * (WIDTH // 128), axis=1)
        for c in range(0, n_lines, WIDTH):
            part = pl.ds(c, WIDTH)
            x, b = react(diffuse(wide, substep[:, part]), bound[:, part], wide_on, wide_off)
            bound[:, part] = b
            propagated[:, part] = diffuse(wide, x)

    def top_moved(t, p):
        f = {19: drug_top[p, 0, 0:8, :]}
        f[20] = jnp.where(lane == 0, pltpu.roll(tops[t, 0], 1, 1), pltpu.roll(drug_top[p, 1, 0:8, :], 1, 1))
        f[21] = jnp.where(lane == 127, pltpu.roll(tops[t, 1], 127, 1), pltpu.roll(drug_top[p, 2, 0:8, :], 127, 1))
        f[22] = drug_top[p, 3, 7:15, :]
        f[23] = drug_top[p, 4, 1:9, :]
        f[24] = own(p, 24, top - 1)[...]
        f[25] = drug_top[p, 5, 0:8, :]
        total = f[19]
        for q in range(20, 26):
            total = total + f[q]
        return f, total

    def wait_tops(t, p):
        for copy in top_copies(t, p):
            copy.wait()

    def wait_flow(t, p):
        wait_edges(t)
        for copy in flow_copies(t, p):
            copy.wait()

    def wait_coupling_sends(t):
        if t == 0:
            wait_bytes(first_in.at[pl.ds(1, n_th - 1)], first_send)
            return
        wait_bytes(table.at[t, pl.ds(1, n_th - 1)], table_send.at[t])
        wait_bytes(sums.at[1, t, pl.ds(1, n_th - 1)], sums_send.at[t])

    collide_all(0, 0)
    wait_bytes(first_in.at[pl.ds(1, n_th - 1)], first_recv)
    line_strut[...] = strut_own
    line_open[...] = PERMEABILITY * (1.0 - strut_own)
    count = first_out[0, 1]
    for o in range(1, n_th):
        count = count + first_in[o, 1]
    line_count[...] = count
    covered = gathered(lambda o, hi: (first_in if o else first_out)[o, 0, hi : hi + 1, :])
    open_row[...] = PERMEABILITY * (1.0 - covered)

    def wall_side(t, p):
        wait_tops(t, p)
        f, total = top_moved(t, p)
        for q in range(19, 26):
            drug_now[q - 19] = f[q]
        drug_now[7] = total
        send_sums(t + 1, total)

    for t in range(STEPS - 1):
        p = t % 2
        wall_flux(t, p)
        wall_first(t, True)
        if p == 1:
            wall_side(t, p)
        wall_second()
        wait_coupling_sends(t)
        wait_flow(t, p)
        collide_all(t + 1, 1 - p)
        if p == 0:
            wall_side(t, p)

    t, p = STEPS - 1, (STEPS - 1) % 2
    wall_flux(t, p)
    wait_flow(t, p)

    def results(rows):
        for r, where in rows:
            flow = None
            for q in Z_UP[:5]:
                term = moved(p, q, r, where) - moved(p, OPPOSITE[q], r, where)
                flow = term if flow is None else flow + term
            axial_out[r] = flow
            if where != "top":
                total = moved(p, 19, r, where)
                for q in range(20, 26):
                    total = total + moved(p, q, r, where)
                drug_out[r] = total

    def results_pair(i, carry):
        results([(2 * i + 1, "middle"), (2 * i + 2, "middle")])
        return carry

    spread_faces(t)
    results([(0, "bottom"), (top, "top")])
    lax.fori_loop(0, (top - 1) // 2, results_pair, 0)
    wall_first(t, False)
    wait_coupling_sends(t)
    wait_tops(t, p)
    drug_out[top] = top_moved(t, p)[1]


def finish(
    substep, bound_in, wide, on_wide, off_wide, drug_in, axial_in,
    drug, axial, free, bound,
    free_part, bound_part, sems,
):
    copies = [
        pltpu.make_async_copy(drug_in, drug, sems.at[0]),
        pltpu.make_async_copy(axial_in, axial, sems.at[1]),
    ]
    for copy in copies:
        copy.start()
    wide_on = jnp.concatenate([on_wide[...]] * (WIDTH // 128), axis=1)
    wide_off = jnp.concatenate([off_wide[...]] * (WIDTH // 128), axis=1)
    for i in range(substep.shape[1] // WIDTH):
        part = pl.ds(i * WIDTH, WIDTH)
        x, b = react(diffuse(wide, substep[:, part]), bound_in[:, part], wide_on, wide_off)
        free_part[:, part] = x
        bound_part[:, part] = b
        for k, (src, dst) in enumerate(((free_part, free), (bound_part, bound))):
            copy = pltpu.make_async_copy(src.at[:, part], dst.at[:, part], sems.at[2 + 2 * i + k])
            copy.start()
            copies.append(copy)
    for copy in copies:
        copy.wait()


def per_device(
    populations, wall_free, wall_bound, wall_propagator, bind_on, bind_off,
    iface_sector, iface_line, strut_mask,
):
    n_th = lax.axis_size("th")
    radial = populations.shape[1]
    vmem = pl.BlockSpec(memory_space=pltpu.VMEM)
    hbm = pl.BlockSpec(memory_space=pltpu.HBM)
    block = (8, 128)
    wall_block = pltpu.VMEM(wall_free.shape, F32)
    scratch = [
        pltpu.VMEM(populations.shape, F32),
        wall_block,
        pltpu.VMEM((128, 128), F32),
        pltpu.VMEM((1, 128), F32),
        pltpu.VMEM((1, 128), F32),
        pltpu.VMEM(block, jnp.int32),
        pltpu.VMEM(block, jnp.int32),
        pltpu.VMEM(block, jnp.int32),
        pltpu.VMEM((7, *block), F32),
        pltpu.VMEM((8, wall_free.shape[1]), F32),
        pltpu.SemaphoreType.DMA((11,)),
        pltpu.VMEM((2, len(MOVING), radial, 16, 128), F32),
        pltpu.VMEM((2, len(STILL), radial, 8, 128), F32),
        pltpu.VMEM((2, 6, 16, 128), F32),
        pltpu.VMEM((8, *block), F32),
        pltpu.VMEM((3, *block), F32),
        pltpu.VMEM((STEPS, 2, *block), F32),
        pltpu.VMEM((STEPS, 2, 24, 128), F32),
        pltpu.VMEM((12, *block), F32),
        pltpu.VMEM((STEPS, 2, *block), F32),
        pltpu.VMEM((8 * n_th, 1024), BF16),
        pltpu.VMEM((128, 1024), BF16),
        pltpu.VMEM(block, jnp.int32),
        pltpu.VMEM(block, jnp.int32),
        pltpu.VMEM(block, F32),
        pltpu.VMEM(block, F32),
        pltpu.VMEM(block, F32),
        pltpu.VMEM(block, F32),
        pltpu.VMEM((STEPS, n_th, *block), F32),
        pltpu.VMEM((2, STEPS, n_th, *block), F32),
        pltpu.VMEM((n_th, 4, *block), F32),
        pltpu.VMEM((n_th, 4, *block), F32),
        pltpu.VMEM(block, F32),
        pltpu.VMEM((128, 128), F32),
        pltpu.VMEM((128, 128), F32),
        wall_block,
        pltpu.SemaphoreType.DMA((STEPS,)),
        pltpu.SemaphoreType.DMA((STEPS,)),
        pltpu.SemaphoreType.DMA((STEPS,)),
        pltpu.SemaphoreType.DMA((STEPS,)),
        pltpu.SemaphoreType.DMA,
        pltpu.SemaphoreType.DMA,
        pltpu.SemaphoreType.DMA((STEPS, 2)),
        pltpu.SemaphoreType.DMA((STEPS, 2)),
        pltpu.SemaphoreType.DMA((STEPS, 6)),
        pltpu.SemaphoreType.DMA((STEPS, 6)),
        pltpu.SemaphoreType.DMA((STEPS, 4)),
        pltpu.SemaphoreType.DMA((STEPS, 4)),
    ]
    field = jax.ShapeDtypeStruct((radial, *block), F32)
    wall = jax.ShapeDtypeStruct(wall_free.shape, F32)
    square = jax.ShapeDtypeStruct((128, 128), F32)
    drug, axial, substep, bound, wide, on_wide, off_wide = pl.pallas_call(
        kernel,
        out_shape=(
            field, field, wall, wall, jax.ShapeDtypeStruct((128, 384), BF16), square, square,
        ),
        in_specs=[hbm] * 9,
        out_specs=(vmem,) * 7,
        scratch_shapes=scratch,
        compiler_params=pltpu.CompilerParams(
            collective_id=0, has_side_effects=True, vmem_limit_bytes=40 * 2**20
        ),
    )(
        *(
            pltpu.with_memory_space_constraint(x, pltpu.HBM)
            for x in (
                populations, wall_free, wall_bound, wall_propagator,
                bind_on.reshape(1, 128), bind_off.reshape(1, 128),
                iface_sector.reshape(block), iface_line.reshape(block), strut_mask.reshape(block),
            )
        )
    )
    return pl.pallas_call(
        finish,
        out_shape=(field, field, wall, wall),
        in_specs=[vmem] * 7,
        out_specs=(hbm,) * 4,
        scratch_shapes=[
            wall_block,
            wall_block,
            pltpu.SemaphoreType.DMA((2 + 2 * (wall_free.shape[1] // WIDTH),)),
        ],
        compiler_params=pltpu.CompilerParams(vmem_limit_bytes=16 * 2**20),
    )(substep, bound, wide, on_wide, off_wide, drug, axial)


def solution(mesh):
    cells = P(None, "th", "ax")
    lines = P(None, ("ax", "th"))
    return jax.shard_map(
        per_device,
        mesh=mesh,
        in_specs=(
            P(None, None, "th", "ax"), lines, lines, P(), P(), P(),
            P(("ax", "th"), None), P(("ax", "th")), P(("ax", "th")),
        ),
        out_specs=(cells, cells, lines, lines),
        check_vma=False,
    )
```

```python
import functools

import jax
import jax.numpy as jnp
from jax import lax
from jax.experimental import pallas as pl
from jax.experimental.pallas import tpu as pltpu
from jax.sharding import PartitionSpec as P

STEPS = 4
RELAX_FLOW = 1.25
RELAX_DRUG = 1.1
PUSH_AXIAL = 0.0001
PERMEABILITY = 0.3
RELEASE_RATE = 0.5

VELOCITIES = [
    (0, 0, 0), (1, 0, 0), (-1, 0, 0), (0, 1, 0), (0, -1, 0), (0, 0, 1), (0, 0, -1),
    (1, 1, 0), (-1, -1, 0), (1, -1, 0), (-1, 1, 0), (1, 0, 1), (-1, 0, -1),
    (1, 0, -1), (-1, 0, 1), (0, 1, 1), (0, -1, -1), (0, 1, -1), (0, -1, 1),
    (0, 0, 0), (1, 0, 0), (-1, 0, 0), (0, 1, 0), (0, -1, 0), (0, 0, 1), (0, 0, -1),
]
OPPOSITE = [0, 2, 1, 4, 3, 6, 5, 8, 7, 10, 9, 12, 11, 14, 13, 16, 15, 18, 17, 19, 21, 20, 23, 22, 25, 24]
MIRROR = [0, 1, 2, 3, 4, 6, 5, 7, 8, 9, 10, 13, 14, 11, 12, 17, 18, 15, 16, 19, 20, 21, 22, 23, 25, 24]

S_UP = [3, 7, 10, 15, 17, 22]
S_DOWN = [4, 8, 9, 16, 18, 23]
MOVING = S_UP + S_DOWN
STILL = [q for q in range(26) if q not in MOVING]
Z_UP = [1, 7, 9, 11, 13, 20]
Z_DOWN = [2, 8, 10, 12, 14, 21]

F32 = jnp.float32
BF16 = jnp.bfloat16
MESH = pl.DeviceIdType.MESH


WIDTH = 256


def diffuse(wide, x):
    x_hi = x.astype(BF16)
    x_lo = (x - x_hi.astype(F32)).astype(BF16)
    return jnp.dot(
        wide[...], jnp.concatenate([x_hi, x_hi, x_lo], axis=0), preferred_element_type=F32
    )


def react(x, b, on, off):
    rate = on * x * (1.0 - b) - off * b
    return x - rate, b + rate


def wait_bytes(ref, sem):
    pltpu.make_async_copy(ref, ref, sem).wait()


def kernel(
    pops_hbm, free_hbm, bound_hbm, prop_hbm, on_hbm, off_hbm, sector_hbm, line_hbm, strut_hbm,
    drug_out, axial_out, substep, bound, wide, on_wide, off_wide,
    pops, free_in, prop, on_row, off_row, sector, line, strut, first_drug, first_free, load_sems,
    moving, still, drug_top, drug_now, speed_top, packed, faces, incoming, tops,
    onehot_hi, onehot_lo, lanes_lo, code_in, open_row, line_open, line_count, line_strut,
    table, sums, first_out, first_in, source,
    from_source, to_surface, propagated,
    table_send, table_recv, sums_send, sums_recv, first_send, first_recv,
    edge_send, edge_recv, flow_send, flow_recv, top_send, top_recv,
):
    n_ax, n_th = lax.axis_size("ax"), lax.axis_size("th")
    ax, th = lax.axis_index("ax"), lax.axis_index("th")
    radial = pops.shape[1]
    top = radial - 1
    lane = lax.broadcasted_iota(jnp.int32, (8, 128), 1)
    ax_up, ax_down = lax.rem(ax + 1, n_ax), lax.rem(ax + n_ax - 1, n_ax)
    th_up, th_down = lax.rem(th + 1, n_th), lax.rem(th + n_th - 1, n_th)

    def peer(offset):
        return (ax, lax.rem(th + offset, n_th))

    beside = [
        (ax_up, th), (ax_down, th),
        (ax_up, th_up), (ax_up, th_down), (ax_down, th_up), (ax_down, th_down),
    ]
    barrier = pltpu.get_barrier_semaphore()
    far_first = sorted(range(1, n_th), key=lambda o: -min(o, n_th - o))
    greeted = [peer(o) for o in far_first] + beside
    for device in greeted:
        pl.semaphore_signal(barrier, inc=1, device_id=device, device_id_type=MESH)

    loads = [
        (sector_hbm, sector), (line_hbm, line), (strut_hbm, strut),
        (pops_hbm.at[19:26, top], first_drug), (free_hbm.at[0:8, :], first_free),
        (prop_hbm, prop), (on_hbm, on_row), (off_hbm, off_row),
        (free_hbm, free_in), (pops_hbm, pops), (bound_hbm, bound),
    ]
    loads = [
        pltpu.make_async_copy(src, dst, load_sems.at[i]) for i, (src, dst) in enumerate(loads)
    ]
    for load in loads:
        load.start()
    for load in loads[:3]:
        load.wait()

    relative = lax.rem(sector[...] - th + n_th, n_th)
    line_all = line[...]
    line_lo = jnp.bitwise_and(line_all, 127)
    line_hi = jnp.right_shift(line_all, 7)
    code_out = relative * 8 + line_hi
    lanes_lo[...] = line_lo
    code_in[...] = lax.rem(n_th - relative, n_th) * 8 + line_hi
    n_blocks = 8 * n_th
    down_blocks = lax.broadcasted_iota(jnp.int32, (n_blocks, 128), 0)
    down_lanes = lax.broadcasted_iota(jnp.int32, (128, 128), 0)
    for s in range(8):
        part = pl.ds(128 * s, 128)
        onehot_hi[:, part] = jnp.where(down_blocks == code_out[s : s + 1, :], 1.0, 0.0).astype(BF16)
        onehot_lo[:, part] = jnp.where(down_lanes == line_lo[s : s + 1, :], 1.0, 0.0).astype(BF16)

    def by_line(values):
        high = values.astype(BF16).astype(F32)
        low = values - high
        total = None
        for s in range(0, 8, 2):
            part = pl.ds(128 * s, 256)
            ones = onehot_hi[:, part]
            rows = []
            for piece in (high, low):
                row = jnp.concatenate([piece[s : s + 1, :], piece[s + 1 : s + 2, :]], axis=1)
                rows.append(ones * row.astype(BF16))
            term = lax.dot_general(
                jnp.concatenate(rows, axis=0),
                onehot_lo[:, part],
                (((1,), (1,)), ((), ())),
                preferred_element_type=F32,
            )
            total = term if total is None else total + term
        return total[:n_blocks] + total[n_blocks:]

    def gathered(block):
        result = jnp.zeros((8, 128), F32)
        where = lanes_lo[...]
        code = code_in[...]
        for o in range(n_th):
            for hi in range(8):
                row = jnp.broadcast_to(block(o, hi), (8, 128))
                found = jnp.take_along_axis(row, where, axis=1, mode="promise_in_bounds")
                result = jnp.where(code == o * 8 + hi, found, result)
        return result

    def table_at(t, o):
        if t > 0:
            return table.at[t, o]
        return first_in.at[o, 2] if o else first_out.at[0, 2]

    def sums_at(t, o):
        if t > 0:
            return sums.at[1 if o else 0, t, o]
        return first_in.at[o, 3] if o else first_out.at[0, 3]

    def table_copy(t, o):
        return pltpu.make_async_remote_copy(
            table.at[t, 0], table.at[t, o], table_send.at[t], table_recv.at[t], peer(o), MESH
        )

    def sums_copy(t, o):
        return pltpu.make_async_remote_copy(
            sums.at[0, t, o], sums.at[1, t, o], sums_send.at[t], sums_recv.at[t], peer(o), MESH
        )

    def first_copy(o):
        return pltpu.make_async_remote_copy(
            first_out.at[o], first_in.at[o], first_send, first_recv, peer(o), MESH
        )

    def send_sums(t, surface):
        found = by_line(surface)
        for o in range(n_th):
            sums[0, t, o] = found[8 * o : 8 * o + 8]
        for o in far_first:
            sums_copy(t, o).start()

    for load in loads[3:5]:
        load.wait()
    strut_own = strut[...].astype(F32)
    surface = first_drug[0]
    for q in range(20, 26):
        surface = surface + first_drug[q - 19]
    found = by_line(surface)
    counts = by_line(jnp.ones((8, 128), F32))
    for o in range(n_th):
        first_out[o, 0] = strut_own
        first_out[o, 1] = counts[8 * o : 8 * o + 8]
        for c in range(8):
            first_out[o, 2, c : c + 1, :] = first_free[0:1, 128 * c : 128 * c + 128]
        first_out[o, 3] = found[8 * o : 8 * o + 8]
    pl.semaphore_wait(barrier, len(greeted))
    for o in far_first:
        first_copy(o).start()
    for q in range(19, 26):
        drug_now[q - 19] = first_drug[q - 19]
    drug_now[7] = surface

    for load in loads[5:]:
        load.wait()
    prop_all = prop[...]
    prop_hi = prop_all.astype(BF16)
    prop_lo = (prop_all - prop_hi.astype(F32)).astype(BF16)
    wide[...] = jnp.concatenate([prop_hi, prop_lo, prop_hi], axis=1)
    from_source[...] = jnp.broadcast_to(prop_all[:, 0:1], (128, 128))
    to_surface[...] = jnp.transpose(jnp.broadcast_to(prop_all[0:1, :], (128, 128)))
    on_wide[...] = jnp.transpose(jnp.broadcast_to(on_row[...], (128, 128)))
    off_wide[...] = jnp.transpose(jnp.broadcast_to(off_row[...], (128, 128)))
    n_lines = free_in.shape[1]
    for c in range(0, n_lines, WIDTH):
        propagated[:, c : c + WIDTH] = diffuse(wide, free_in[:, c : c + WIDTH])

    def own(p, q, r):
        if q in S_UP:
            return moving.at[p, MOVING.index(q), r, 8:16, :]
        if q in S_DOWN:
            return moving.at[p, MOVING.index(q), r, 0:8, :]
        return still.at[p, STILL.index(q), r]

    def shifted_s(p, q, r):
        if q in S_UP:
            return moving[p, MOVING.index(q), r, 7:15, :]
        if q in S_DOWN:
            return moving[p, MOVING.index(q), r, 1:9, :]
        return still[p, STILL.index(q), r]

    def spread_faces(t):
        for side, members in enumerate((Z_UP, Z_DOWN)):
            for k, q in enumerate(members):
                first = 8 - VELOCITIES[q][1]
                face = faces[t, side, first : first + 8, :]
                incoming[6 * side + k] = pltpu.roll(face, (128 - 16 * k) % 128, 1)

    def pack_faces(t, p):
        for side, members in enumerate((Z_UP, Z_DOWN)):
            block = jnp.zeros((8, 128), F32)
            for k, q in enumerate(members):
                face = jnp.zeros((8, 128), F32)
                for r in range(top + 1 if q < 19 else top):
                    face = jnp.where(lane == r + 1, own(p, q, r)[...], face)
                block = block + pltpu.roll(face, 16 * k, 1)
            packed[t, side] = block

    def pulled(p, q, r):
        value = shifted_s(p, q, r)
        if q in Z_UP:
            value = jnp.where(lane == r + 1, incoming[Z_UP.index(q)], value)
            return pltpu.roll(value, 127 - r, 1)
        if q in Z_DOWN:
            value = jnp.where(lane == r + 1, incoming[6 + Z_DOWN.index(q)], value)
            return pltpu.roll(value, 126 - r, 1)
        return value

    def own_plain(p, q, r):
        if q in Z_UP:
            return pltpu.roll(own(p, q, r)[...], 126 - r, 1)
        if q in Z_DOWN:
            return pltpu.roll(own(p, q, r)[...], 127 - r, 1)
        return own(p, q, r)[...]

    def moved(p, q, r, where):
        step_r = VELOCITIES[q][2]
        if step_r == 1 and where == "bottom":
            return pulled(p, MIRROR[q], r)
        if step_r == -1 and where == "top":
            return own_plain(p, OPPOSITE[q], r)
        return pulled(p, q, r - step_r)

    def collide_flow(f):
        d = {q: f[q] - f[q + 1] for q in (1, 3, 5, 7, 9, 11, 13, 15, 17)}
        density = f[0]
        for q in range(1, 19):
            density = density + f[q]
        jz = d[1] + d[7] + d[9] + d[11] + d[13] + PUSH_AXIAL
        js = d[3] + d[7] - d[9] + d[15] + d[17]
        jr = d[5] + d[11] - d[13] + d[15] - d[17]
        uz, us, ur = jz / density, js / density, jr / density
        base = 1.0 - 1.5 * (uz * uz + us * us + ur * ur)
        edge = density * (RELAX_FLOW / 36.0)
        face = density * (RELAX_FLOW / 18.0)
        keep = 1.0 - RELAX_FLOW
        post = {0: keep * f[0] + density * (RELAX_FLOW / 3.0) * base}
        along = {
            1: uz, 3: us, 5: ur, 7: uz + us, 9: uz - us,
            11: uz + ur, 13: uz - ur, 15: us + ur, 17: us - ur,
        }
        for q, speed in along.items():
            weight = face if q < 7 else edge
            even = weight * (base + 4.5 * speed * speed)
            odd = weight * (3.0 * speed)
            post[q] = keep * f[q] + (even + odd)
            post[q + 1] = keep * f[q + 1] + (even - odd)
        return post, (uz, us, ur)

    def collide_drug(f, total, speeds):
        keep = 1.0 - RELAX_DRUG
        share = total * (RELAX_DRUG * 0.125)
        post = {19: keep * f[19] + 2.0 * share}
        for q, speed in zip((20, 22, 24), speeds):
            odd = 4.0 * speed
            post[q] = keep * f[q] + share * (1.0 + odd)
            post[q + 1] = keep * f[q + 1] + share * (1.0 - odd)
        return post

    def layers(read, p, rows):
        loaded = []
        for r, where in rows:
            members = range(19 if where == "top" else 26)
            loaded.append({q: read(q, r, where) for q in members})
        posts = []
        for (_, where), f in zip(rows, loaded):
            post, speeds = collide_flow(f)
            if where == "top":
                for i in range(3):
                    speed_top[i] = speeds[i]
            else:
                total = f[19]
                for q in range(20, 26):
                    total = total + f[q]
                post.update(collide_drug(f, total, speeds))
            posts.append(post)
        for (r, _), post in zip(rows, posts):
            for q, value in post.items():
                if q in Z_UP:
                    value = pltpu.roll(value, r + 2, 1)
                elif q in Z_DOWN:
                    value = pltpu.roll(value, r + 1, 1)
                own(p, q, r)[...] = value

    def flow_copies(t, p):
        def copy(src, dst, device, i):
            return pltpu.make_async_remote_copy(
                src, dst, flow_send.at[t, i], flow_recv.at[t, i], device, MESH
            )

        copies = []
        for side, to in ((0, ax_up), (1, ax_down)):
            i = 3 * side
            copies += [
                copy(packed.at[t, side], faces.at[t, side, 8:16, :], (to, th), i),
                copy(packed.at[t, side, 7:8, :], faces.at[t, side, 7:8, :], (to, th_up), i + 1),
                copy(packed.at[t, side, 0:1, :], faces.at[t, side, 16:17, :], (to, th_down), i + 2),
            ]
        return copies

    def send_edges(t, p, r, count, members):
        rows = pl.ds(r, count)
        for side, first, src, dst, to in ((0, 0, 15, 7, th_up), (1, 6, 0, 8, th_down)):
            movers = pl.ds(first, members)
            pltpu.make_async_remote_copy(
                moving.at[p, movers, rows, src, :], moving.at[p, movers, rows, dst, :],
                edge_send.at[t, side], edge_recv.at[t, side], (ax, to), MESH,
            ).start()

    def wait_edges(t):
        all_rows = pops.at[0:19, 0:5, 0, :]
        assert 19 * 5 == 6 * top + 5
        for side in range(2):
            wait_bytes(all_rows, edge_send.at[t, side])
            wait_bytes(all_rows, edge_recv.at[t, side])

    def collide_all(t, p):
        if t == 0:
            read = lambda q, r, where: pops[q, r]
        else:
            spread_faces(t - 1)
            read = functools.partial(moved, 1 - p)
        layers(read, p, [(0, "bottom"), (top, "top")])
        send_edges(t, p, 0, 1, 6)
        send_edges(t, p, top, 1, 5)

        def pair(i, carry):
            layers(read, p, [(2 * i + 1, "middle"), (2 * i + 2, "middle")])
            send_edges(t, p, 2 * i + 1, 2, 6)
            return carry

        lax.fori_loop(0, (top - 1) // 2, pair, 0)
        pack_faces(t, p)
        for copy in flow_copies(t, p):
            copy.start()

    def top_copies(t, p):
        def copy(src, dst, device, i):
            return pltpu.make_async_remote_copy(
                src, dst, top_send.at[t, i], top_recv.at[t, i], device, MESH
            )

        return [
            copy(drug_top.at[p, 1, 0:8, :], tops.at[t, 0], (ax_up, th), 0),
            copy(drug_top.at[p, 2, 0:8, :], tops.at[t, 1], (ax_down, th), 1),
            copy(drug_top.at[p, 3, 15, :], drug_top.at[p, 3, 7, :], (ax, th_up), 2),
            copy(drug_top.at[p, 4, 0, :], drug_top.at[p, 4, 8, :], (ax, th_down), 3),
        ]

    def wall_flux(t, p):
        if t > 0:
            wait_bytes(table.at[t, pl.ds(1, n_th - 1)], table_recv.at[t])
        free_rows = gathered(lambda o, hi: table_at(t, o)[hi : hi + 1, :])
        surface = drug_now[7]
        flux = open_row[...] * (surface - free_rows)
        lowered = {19: drug_now[0] - 0.25 * flux}
        for q in range(20, 26):
            lowered[q] = drug_now[q - 19] - 0.125 * flux
        post = collide_drug(lowered, surface - flux, [speed_top[i] for i in range(3)])
        drug_top[p, 1, 0:8, :] = post[20]
        drug_top[p, 2, 0:8, :] = post[21]
        drug_top[p, 3, 8:16, :] = post[22]
        drug_top[p, 4, 0:8, :] = post[23]
        for copy in top_copies(t, p):
            copy.start()
        drug_top[p, 0, 0:8, :] = post[19]
        drug_top[p, 5, 0:8, :] = post[24]
        own(p, 25, top)[...] = post[25]

    def wall_first(t, send):
        if t > 0:
            wait_bytes(sums.at[1, t, pl.ds(1, n_th - 1)], sums_recv.at[t])
        total = sums_at(t, 0)[...]
        for o in range(1, n_th):
            total = total + sums_at(t, o)[...]
        flux = line_open[...] * (total - line_count[...] * table_at(t, 0)[...])
        source[...] = flux + RELEASE_RATE * line_strut[...]
        for c in range(8):
            part = pl.ds(128 * c, 128)
            x = propagated[:, part] + from_source[...] * source[c : c + 1, :]
            x, b = react(x, bound[:, part], on_wide[...], off_wide[...])
            substep[:, part] = x
            bound[:, part] = b
            if send:
                x = jnp.sum(to_surface[...] * x, axis=0, keepdims=True)
                x, _ = react(x, b[0:1, :], on_wide[0:1, :], off_wide[0:1, :])
                table[t + 1, 0, c : c + 1, :] = x
        if send:
            for o in far_first:
                table_copy(t + 1, o).start()

    def wall_second():
        wide_on = jnp.concatenate([on_wide[...]] * (WIDTH // 128), axis=1)
        wide_off = jnp.concatenate([off_wide[...]] * (WIDTH // 128), axis=1)
        for c in range(0, n_lines, WIDTH):
            part = pl.ds(c, WIDTH)
            x, b = react(diffuse(wide, substep[:, part]), bound[:, part], wide_on, wide_off)
            bound[:, part] = b
            propagated[:, part] = diffuse(wide, x)

    def top_moved(t, p):
        f = {19: drug_top[p, 0, 0:8, :]}
        f[20] = jnp.where(lane == 0, pltpu.roll(tops[t, 0], 1, 1), pltpu.roll(drug_top[p, 1, 0:8, :], 1, 1))
        f[21] = jnp.where(lane == 127, pltpu.roll(tops[t, 1], 127, 1), pltpu.roll(drug_top[p, 2, 0:8, :], 127, 1))
        f[22] = drug_top[p, 3, 7:15, :]
        f[23] = drug_top[p, 4, 1:9, :]
        f[24] = own(p, 24, top - 1)[...]
        f[25] = drug_top[p, 5, 0:8, :]
        total = f[19]
        for q in range(20, 26):
            total = total + f[q]
        return f, total

    def wait_tops(t, p):
        for copy in top_copies(t, p):
            copy.wait()

    def wait_flow(t, p):
        wait_edges(t)
        for copy in flow_copies(t, p):
            copy.wait()

    def wait_coupling_sends(t):
        if t == 0:
            wait_bytes(first_in.at[pl.ds(1, n_th - 1)], first_send)
            return
        wait_bytes(table.at[t, pl.ds(1, n_th - 1)], table_send.at[t])
        wait_bytes(sums.at[1, t, pl.ds(1, n_th - 1)], sums_send.at[t])

    collide_all(0, 0)
    wait_bytes(first_in.at[pl.ds(1, n_th - 1)], first_recv)
    line_strut[...] = strut_own
    line_open[...] = PERMEABILITY * (1.0 - strut_own)
    count = first_out[0, 1]
    for o in range(1, n_th):
        count = count + first_in[o, 1]
    line_count[...] = count
    covered = gathered(lambda o, hi: (first_in if o else first_out)[o, 0, hi : hi + 1, :])
    open_row[...] = PERMEABILITY * (1.0 - covered)

    def wall_side(t, p):
        wait_tops(t, p)
        f, total = top_moved(t, p)
        for q in range(19, 26):
            drug_now[q - 19] = f[q]
        drug_now[7] = total
        send_sums(t + 1, total)

    for t in range(STEPS - 1):
        p = t % 2
        wall_flux(t, p)
        wall_first(t, True)
        if p == 1:
            wall_side(t, p)
        wall_second()
        wait_coupling_sends(t)
        wait_flow(t, p)
        collide_all(t + 1, 1 - p)
        if p == 0:
            wall_side(t, p)

    t, p = STEPS - 1, (STEPS - 1) % 2
    wall_flux(t, p)
    wait_flow(t, p)

    def results(rows):
        for r, where in rows:
            flow = None
            for q in Z_UP[:5]:
                term = moved(p, q, r, where) - moved(p, OPPOSITE[q], r, where)
                flow = term if flow is None else flow + term
            axial_out[r] = flow
            if where != "top":
                total = moved(p, 19, r, where)
                for q in range(20, 26):
                    total = total + moved(p, q, r, where)
                drug_out[r] = total

    def results_pair(i, carry):
        results([(2 * i + 1, "middle"), (2 * i + 2, "middle")])
        return carry

    spread_faces(t)
    results([(0, "bottom"), (top, "top")])
    lax.fori_loop(0, (top - 1) // 2, results_pair, 0)
    wall_first(t, False)
    wait_coupling_sends(t)
    wait_tops(t, p)
    drug_out[top] = top_moved(t, p)[1]


def finish(
    substep, bound_in, wide, on_wide, off_wide, drug_in, axial_in,
    drug, axial, free, bound,
    free_part, bound_part, sems,
):
    copies = [
        pltpu.make_async_copy(drug_in, drug, sems.at[0]),
        pltpu.make_async_copy(axial_in, axial, sems.at[1]),
    ]
    for copy in copies:
        copy.start()
    wide_on = jnp.concatenate([on_wide[...]] * (WIDTH // 128), axis=1)
    wide_off = jnp.concatenate([off_wide[...]] * (WIDTH // 128), axis=1)
    for i in range(substep.shape[1] // WIDTH):
        part = pl.ds(i * WIDTH, WIDTH)
        x, b = react(diffuse(wide, substep[:, part]), bound_in[:, part], wide_on, wide_off)
        free_part[:, part] = x
        bound_part[:, part] = b
        for k, (src, dst) in enumerate(((free_part, free), (bound_part, bound))):
            copy = pltpu.make_async_copy(src.at[:, part], dst.at[:, part], sems.at[2 + 2 * i + k])
            copy.start()
            copies.append(copy)
    for copy in copies:
        copy.wait()


def per_device(
    populations, wall_free, wall_bound, wall_propagator, bind_on, bind_off,
    iface_sector, iface_line, strut_mask,
):
    n_th = lax.axis_size("th")
    radial = populations.shape[1]
    vmem = pl.BlockSpec(memory_space=pltpu.VMEM)
    hbm = pl.BlockSpec(memory_space=pltpu.HBM)
    block = (8, 128)
    wall_block = pltpu.VMEM(wall_free.shape, F32)
    scratch = [
        pltpu.VMEM(populations.shape, F32),
        wall_block,
        pltpu.VMEM((128, 128), F32),
        pltpu.VMEM((1, 128), F32),
        pltpu.VMEM((1, 128), F32),
        pltpu.VMEM(block, jnp.int32),
        pltpu.VMEM(block, jnp.int32),
        pltpu.VMEM(block, jnp.int32),
        pltpu.VMEM((7, *block), F32),
        pltpu.VMEM((8, wall_free.shape[1]), F32),
        pltpu.SemaphoreType.DMA((11,)),
        pltpu.VMEM((2, len(MOVING), radial, 16, 128), F32),
        pltpu.VMEM((2, len(STILL), radial, 8, 128), F32),
        pltpu.VMEM((2, 6, 16, 128), F32),
        pltpu.VMEM((8, *block), F32),
        pltpu.VMEM((3, *block), F32),
        pltpu.VMEM((STEPS, 2, *block), F32),
        pltpu.VMEM((STEPS, 2, 24, 128), F32),
        pltpu.VMEM((12, *block), F32),
        pltpu.VMEM((STEPS, 2, *block), F32),
        pltpu.VMEM((8 * n_th, 1024), BF16),
        pltpu.VMEM((128, 1024), BF16),
        pltpu.VMEM(block, jnp.int32),
        pltpu.VMEM(block, jnp.int32),
        pltpu.VMEM(block, F32),
        pltpu.VMEM(block, F32),
        pltpu.VMEM(block, F32),
        pltpu.VMEM(block, F32),
        pltpu.VMEM((STEPS, n_th, *block), F32),
        pltpu.VMEM((2, STEPS, n_th, *block), F32),
        pltpu.VMEM((n_th, 4, *block), F32),
        pltpu.VMEM((n_th, 4, *block), F32),
        pltpu.VMEM(block, F32),
        pltpu.VMEM((128, 128), F32),
        pltpu.VMEM((128, 128), F32),
        wall_block,
        pltpu.SemaphoreType.DMA((STEPS,)),
        pltpu.SemaphoreType.DMA((STEPS,)),
        pltpu.SemaphoreType.DMA((STEPS,)),
        pltpu.SemaphoreType.DMA((STEPS,)),
        pltpu.SemaphoreType.DMA,
        pltpu.SemaphoreType.DMA,
        pltpu.SemaphoreType.DMA((STEPS, 2)),
        pltpu.SemaphoreType.DMA((STEPS, 2)),
        pltpu.SemaphoreType.DMA((STEPS, 6)),
        pltpu.SemaphoreType.DMA((STEPS, 6)),
        pltpu.SemaphoreType.DMA((STEPS, 4)),
        pltpu.SemaphoreType.DMA((STEPS, 4)),
    ]
    field = jax.ShapeDtypeStruct((radial, *block), F32)
    wall = jax.ShapeDtypeStruct(wall_free.shape, F32)
    square = jax.ShapeDtypeStruct((128, 128), F32)
    drug, axial, substep, bound, wide, on_wide, off_wide = pl.pallas_call(
        kernel,
        out_shape=(
            field, field, wall, wall, jax.ShapeDtypeStruct((128, 384), BF16), square, square,
        ),
        in_specs=[hbm] * 9,
        out_specs=(vmem,) * 7,
        scratch_shapes=scratch,
        compiler_params=pltpu.CompilerParams(
            collective_id=0, has_side_effects=True, vmem_limit_bytes=40 * 2**20
        ),
    )(
        *(
            pltpu.with_memory_space_constraint(x, pltpu.HBM)
            for x in (
                populations, wall_free, wall_bound, wall_propagator,
                bind_on.reshape(1, 128), bind_off.reshape(1, 128),
                iface_sector.reshape(block), iface_line.reshape(block), strut_mask.reshape(block),
            )
        )
    )
    return pl.pallas_call(
        finish,
        out_shape=(field, field, wall, wall),
        in_specs=[vmem] * 7,
        out_specs=(hbm,) * 4,
        scratch_shapes=[
            wall_block,
            wall_block,
            pltpu.SemaphoreType.DMA((2 + 2 * (wall_free.shape[1] // WIDTH),)),
        ],
        compiler_params=pltpu.CompilerParams(vmem_limit_bytes=16 * 2**20),
    )(substep, bound, wide, on_wide, off_wide, drug, axial)


def solution(mesh):
    cells = P(None, "th", "ax")
    lines = P(None, ("ax", "th"))
    return jax.shard_map(
        per_device,
        mesh=mesh,
        in_specs=(
            P(None, None, "th", "ax"), lines, lines, P(), P(), P(),
            P(("ax", "th"), None), P(("ax", "th")), P(("ax", "th")),
        ),
        out_specs=(cells, cells, lines, lines),
        check_vma=False,
    )
```

```python
import functools

import jax
import jax.numpy as jnp
from jax import lax
from jax.experimental import pallas as pl
from jax.experimental.pallas import tpu as pltpu
from jax.sharding import PartitionSpec as P

STEPS = 4
RELAX_FLOW = 1.25
RELAX_DRUG = 1.1
PUSH_AXIAL = 0.0001
PERMEABILITY = 0.3
RELEASE_RATE = 0.5

VELOCITIES = [
    (0, 0, 0), (1, 0, 0), (-1, 0, 0), (0, 1, 0), (0, -1, 0), (0, 0, 1), (0, 0, -1),
    (1, 1, 0), (-1, -1, 0), (1, -1, 0), (-1, 1, 0), (1, 0, 1), (-1, 0, -1),
    (1, 0, -1), (-1, 0, 1), (0, 1, 1), (0, -1, -1), (0, 1, -1), (0, -1, 1),
    (0, 0, 0), (1, 0, 0), (-1, 0, 0), (0, 1, 0), (0, -1, 0), (0, 0, 1), (0, 0, -1),
]
OPPOSITE = [0, 2, 1, 4, 3, 6, 5, 8, 7, 10, 9, 12, 11, 14, 13, 16, 15, 18, 17, 19, 21, 20, 23, 22, 25, 24]
MIRROR = [0, 1, 2, 3, 4, 6, 5, 7, 8, 9, 10, 13, 14, 11, 12, 17, 18, 15, 16, 19, 20, 21, 22, 23, 25, 24]

S_UP = [3, 7, 10, 15, 17, 22]
S_DOWN = [4, 8, 9, 16, 18, 23]
MOVING = S_UP + S_DOWN
STILL = [q for q in range(26) if q not in MOVING]
Z_UP = [1, 7, 9, 11, 13, 20]
Z_DOWN = [2, 8, 10, 12, 14, 21]

F32 = jnp.float32
BF16 = jnp.bfloat16
MESH = pl.DeviceIdType.MESH


WIDTH = 256


def diffuse(wide, x):
    x_hi = x.astype(BF16)
    x_lo = (x - x_hi.astype(F32)).astype(BF16)
    return jnp.dot(
        wide[...], jnp.concatenate([x_hi, x_hi, x_lo], axis=0), preferred_element_type=F32
    )


def react(x, b, on, off):
    rate = on * x * (1.0 - b) - off * b
    return x - rate, b + rate


def wait_bytes(ref, sem):
    pltpu.make_async_copy(ref, ref, sem).wait()


def kernel(
    pops_hbm, free_hbm, bound_hbm, prop_hbm, on_hbm, off_hbm, sector_hbm, line_hbm, strut_hbm,
    drug_out, axial_out, substep, bound, wide, on_wide, off_wide,
    pops, free_in, prop, on_row, off_row, sector, line, strut, first_drug, first_free, load_sems,
    moving, still, drug_top, drug_now, speed_top, packed, faces, incoming, tops,
    onehot_hi, onehot_lo, lanes_lo, code_in, open_row, line_open, line_count, line_strut,
    table, sums, first_out, first_in, source,
    from_source, to_surface, through, response, propagated,
    table_send, table_recv, sums_send, sums_recv, first_send, first_recv,
    edge_send, edge_recv, flow_send, flow_recv, top_send, top_recv,
):
    n_ax, n_th = lax.axis_size("ax"), lax.axis_size("th")
    ax, th = lax.axis_index("ax"), lax.axis_index("th")
    radial = pops.shape[1]
    top = radial - 1
    lane = lax.broadcasted_iota(jnp.int32, (8, 128), 1)
    ax_up, ax_down = lax.rem(ax + 1, n_ax), lax.rem(ax + n_ax - 1, n_ax)
    th_up, th_down = lax.rem(th + 1, n_th), lax.rem(th + n_th - 1, n_th)

    def peer(offset):
        return (ax, lax.rem(th + offset, n_th))

    beside = [
        (ax_up, th), (ax_down, th),
        (ax_up, th_up), (ax_up, th_down), (ax_down, th_up), (ax_down, th_down),
    ]
    barrier = pltpu.get_barrier_semaphore()
    far_first = sorted(range(1, n_th), key=lambda o: -min(o, n_th - o))
    greeted = [peer(o) for o in far_first] + beside
    for device in greeted:
        pl.semaphore_signal(barrier, inc=1, device_id=device, device_id_type=MESH)

    loads = [
        (sector_hbm, sector), (line_hbm, line), (strut_hbm, strut),
        (pops_hbm.at[19:26, top], first_drug), (free_hbm.at[0:8, :], first_free),
        (prop_hbm, prop), (on_hbm, on_row), (off_hbm, off_row),
        (free_hbm, free_in), (pops_hbm, pops), (bound_hbm, bound),
    ]
    loads = [
        pltpu.make_async_copy(src, dst, load_sems.at[i]) for i, (src, dst) in enumerate(loads)
    ]
    for load in loads:
        load.start()
    for load in loads[:3]:
        load.wait()

    relative = lax.rem(sector[...] - th + n_th, n_th)
    line_all = line[...]
    line_lo = jnp.bitwise_and(line_all, 127)
    line_hi = jnp.right_shift(line_all, 7)
    code_out = relative * 8 + line_hi
    lanes_lo[...] = line_lo
    code_in[...] = lax.rem(n_th - relative, n_th) * 8 + line_hi
    n_blocks = 8 * n_th
    down_blocks = lax.broadcasted_iota(jnp.int32, (n_blocks, 128), 0)
    down_lanes = lax.broadcasted_iota(jnp.int32, (128, 128), 0)
    for s in range(8):
        part = pl.ds(128 * s, 128)
        onehot_hi[:, part] = jnp.where(down_blocks == code_out[s : s + 1, :], 1.0, 0.0).astype(BF16)
        onehot_lo[:, part] = jnp.where(down_lanes == line_lo[s : s + 1, :], 1.0, 0.0).astype(BF16)

    def by_line(values):
        high = values.astype(BF16).astype(F32)
        low = values - high
        total = None
        for s in range(0, 8, 2):
            part = pl.ds(128 * s, 256)
            ones = onehot_hi[:, part]
            rows = []
            for piece in (high, low):
                row = jnp.concatenate([piece[s : s + 1, :], piece[s + 1 : s + 2, :]], axis=1)
                rows.append(ones * row.astype(BF16))
            term = lax.dot_general(
                jnp.concatenate(rows, axis=0),
                onehot_lo[:, part],
                (((1,), (1,)), ((), ())),
                preferred_element_type=F32,
            )
            total = term if total is None else total + term
        return total[:n_blocks] + total[n_blocks:]

    def gathered(block):
        result = jnp.zeros((8, 128), F32)
        where = lanes_lo[...]
        code = code_in[...]
        for o in range(n_th):
            for hi in range(8):
                row = jnp.broadcast_to(block(o, hi), (8, 128))
                found = jnp.take_along_axis(row, where, axis=1, mode="promise_in_bounds")
                result = jnp.where(code == o * 8 + hi, found, result)
        return result

    def table_at(t, o):
        if t > 0:
            return table.at[t, o]
        return first_in.at[o, 2] if o else first_out.at[0, 2]

    def sums_at(t, o):
        if t > 0:
            return sums.at[1 if o else 0, t, o]
        return first_in.at[o, 3] if o else first_out.at[0, 3]

    def table_copy(t, o):
        return pltpu.make_async_remote_copy(
            table.at[t, 0], table.at[t, o], table_send.at[t], table_recv.at[t], peer(o), MESH
        )

    def sums_copy(t, o):
        return pltpu.make_async_remote_copy(
            sums.at[0, t, o], sums.at[1, t, o], sums_send.at[t], sums_recv.at[t], peer(o), MESH
        )

    def first_copy(o):
        return pltpu.make_async_remote_copy(
            first_out.at[o], first_in.at[o], first_send, first_recv, peer(o), MESH
        )

    def send_sums(t, surface):
        found = by_line(surface)
        for o in range(n_th):
            sums[0, t, o] = found[8 * o : 8 * o + 8]
        for o in far_first:
            sums_copy(t, o).start()

    for load in loads[3:5]:
        load.wait()
    strut_own = strut[...].astype(F32)
    surface = first_drug[0]
    for q in range(20, 26):
        surface = surface + first_drug[q - 19]
    found = by_line(surface)
    counts = by_line(jnp.ones((8, 128), F32))
    for o in range(n_th):
        first_out[o, 0] = strut_own
        first_out[o, 1] = counts[8 * o : 8 * o + 8]
        for c in range(8):
            first_out[o, 2, c : c + 1, :] = first_free[0:1, 128 * c : 128 * c + 128]
        first_out[o, 3] = found[8 * o : 8 * o + 8]
    pl.semaphore_wait(barrier, len(greeted))
    for o in far_first:
        first_copy(o).start()
    for q in range(19, 26):
        drug_now[q - 19] = first_drug[q - 19]
    drug_now[7] = surface

    for load in loads[5:]:
        load.wait()
    prop_all = prop[...]
    prop_hi = prop_all.astype(BF16)
    prop_lo = (prop_all - prop_hi.astype(F32)).astype(BF16)
    wide[...] = jnp.concatenate([prop_hi, prop_lo, prop_hi], axis=1)
    from_source[...] = jnp.broadcast_to(prop_all[:, 0:1], (128, 128))
    to_surface[...] = jnp.transpose(jnp.broadcast_to(prop_all[0:1, :], (128, 128)))
    on_wide[...] = jnp.transpose(jnp.broadcast_to(on_row[...], (128, 128)))
    off_wide[...] = jnp.transpose(jnp.broadcast_to(off_row[...], (128, 128)))
    n_lines = free_in.shape[1]
    for c in range(0, n_lines, WIDTH):
        propagated[:, c : c + WIDTH] = diffuse(wide, free_in[:, c : c + WIDTH])

    def own(p, q, r):
        if q in S_UP:
            return moving.at[p, MOVING.index(q), r, 8:16, :]
        if q in S_DOWN:
            return moving.at[p, MOVING.index(q), r, 0:8, :]
        return still.at[p, STILL.index(q), r]

    def shifted_s(p, q, r):
        if q in S_UP:
            return moving[p, MOVING.index(q), r, 7:15, :]
        if q in S_DOWN:
            return moving[p, MOVING.index(q), r, 1:9, :]
        return still[p, STILL.index(q), r]

    def spread_faces(t):
        for side, members in enumerate((Z_UP, Z_DOWN)):
            for k, q in enumerate(members):
                first = 8 - VELOCITIES[q][1]
                face = faces[t, side, first : first + 8, :]
                incoming[6 * side + k] = pltpu.roll(face, (128 - 16 * k) % 128, 1)

    def pack_faces(t, p):
        for side, members in enumerate((Z_UP, Z_DOWN)):
            block = jnp.zeros((8, 128), F32)
            for k, q in enumerate(members):
                face = jnp.zeros((8, 128), F32)
                for r in range(top + 1 if q < 19 else top):
                    face = jnp.where(lane == r + 1, own(p, q, r)[...], face)
                block = block + pltpu.roll(face, 16 * k, 1)
            packed[t, side] = block

    def pulled(p, q, r):
        value = shifted_s(p, q, r)
        if q in Z_UP:
            value = jnp.where(lane == r + 1, incoming[Z_UP.index(q)], value)
            return pltpu.roll(value, 127 - r, 1)
        if q in Z_DOWN:
            value = jnp.where(lane == r + 1, incoming[6 + Z_DOWN.index(q)], value)
            return pltpu.roll(value, 126 - r, 1)
        return value

    def own_plain(p, q, r):
        if q in Z_UP:
            return pltpu.roll(own(p, q, r)[...], 126 - r, 1)
        if q in Z_DOWN:
            return pltpu.roll(own(p, q, r)[...], 127 - r, 1)
        return own(p, q, r)[...]

    def moved(p, q, r, where):
        step_r = VELOCITIES[q][2]
        if step_r == 1 and where == "bottom":
            return pulled(p, MIRROR[q], r)
        if step_r == -1 and where == "top":
            return own_plain(p, OPPOSITE[q], r)
        return pulled(p, q, r - step_r)

    def collide_flow(f):
        d = {q: f[q] - f[q + 1] for q in (1, 3, 5, 7, 9, 11, 13, 15, 17)}
        density = f[0]
        for q in range(1, 19):
            density = density + f[q]
        jz = d[1] + d[7] + d[9] + d[11] + d[13] + PUSH_AXIAL
        js = d[3] + d[7] - d[9] + d[15] + d[17]
        jr = d[5] + d[11] - d[13] + d[15] - d[17]
        uz, us, ur = jz / density, js / density, jr / density
        base = 1.0 - 1.5 * (uz * uz + us * us + ur * ur)
        edge = density * (RELAX_FLOW / 36.0)
        face = density * (RELAX_FLOW / 18.0)
        keep = 1.0 - RELAX_FLOW
        post = {0: keep * f[0] + density * (RELAX_FLOW / 3.0) * base}
        along = {
            1: uz, 3: us, 5: ur, 7: uz + us, 9: uz - us,
            11: uz + ur, 13: uz - ur, 15: us + ur, 17: us - ur,
        }
        for q, speed in along.items():
            weight = face if q < 7 else edge
            even = weight * (base + 4.5 * speed * speed)
            odd = weight * (3.0 * speed)
            post[q] = keep * f[q] + (even + odd)
            post[q + 1] = keep * f[q + 1] + (even - odd)
        return post, (uz, us, ur)

    def collide_drug(f, total, speeds):
        keep = 1.0 - RELAX_DRUG
        share = total * (RELAX_DRUG * 0.125)
        post = {19: keep * f[19] + 2.0 * share}
        for q, speed in zip((20, 22, 24), speeds):
            odd = 4.0 * speed
            post[q] = keep * f[q] + share * (1.0 + odd)
            post[q + 1] = keep * f[q + 1] + share * (1.0 - odd)
        return post

    def layers(read, p, rows):
        loaded = []
        for r, where in rows:
            members = range(19 if where == "top" else 26)
            loaded.append({q: read(q, r, where) for q in members})
        posts = []
        for (_, where), f in zip(rows, loaded):
            post, speeds = collide_flow(f)
            if where == "top":
                for i in range(3):
                    speed_top[i] = speeds[i]
            else:
                total = f[19]
                for q in range(20, 26):
                    total = total + f[q]
                post.update(collide_drug(f, total, speeds))
            posts.append(post)
        for (r, _), post in zip(rows, posts):
            for q, value in post.items():
                if q in Z_UP:
                    value = pltpu.roll(value, r + 2, 1)
                elif q in Z_DOWN:
                    value = pltpu.roll(value, r + 1, 1)
                own(p, q, r)[...] = value

    def flow_copies(t, p):
        def copy(src, dst, device, i):
            return pltpu.make_async_remote_copy(
                src, dst, flow_send.at[t, i], flow_recv.at[t, i], device, MESH
            )

        copies = []
        for side, to in ((0, ax_up), (1, ax_down)):
            i = 3 * side
            copies += [
                copy(packed.at[t, side], faces.at[t, side, 8:16, :], (to, th), i),
                copy(packed.at[t, side, 7:8, :], faces.at[t, side, 7:8, :], (to, th_up), i + 1),
                copy(packed.at[t, side, 0:1, :], faces.at[t, side, 16:17, :], (to, th_down), i + 2),
            ]
        return copies

    def send_edges(t, p, r, count, members):
        rows = pl.ds(r, count)
        for side, first, src, dst, to in ((0, 0, 15, 7, th_up), (1, 6, 0, 8, th_down)):
            movers = pl.ds(first, members)
            pltpu.make_async_remote_copy(
                moving.at[p, movers, rows, src, :], moving.at[p, movers, rows, dst, :],
                edge_send.at[t, side], edge_recv.at[t, side], (ax, to), MESH,
            ).start()

    def wait_edges(t):
        all_rows = pops.at[0:19, 0:5, 0, :]
        assert 19 * 5 == 6 * top + 5
        for side in range(2):
            wait_bytes(all_rows, edge_send.at[t, side])
            wait_bytes(all_rows, edge_recv.at[t, side])

    def collide_all(t, p):
        if t == 0:
            read = lambda q, r, where: pops[q, r]
        else:
            spread_faces(t - 1)
            read = functools.partial(moved, 1 - p)
        layers(read, p, [(0, "bottom"), (top, "top")])
        send_edges(t, p, 0, 1, 6)
        send_edges(t, p, top, 1, 5)

        def pair(i, carry):
            layers(read, p, [(2 * i + 1, "middle"), (2 * i + 2, "middle")])
            send_edges(t, p, 2 * i + 1, 2, 6)
            return carry

        lax.fori_loop(0, (top - 1) // 2, pair, 0)
        pack_faces(t, p)
        for copy in flow_copies(t, p):
            copy.start()

    def top_copies(t, p):
        def copy(src, dst, device, i):
            return pltpu.make_async_remote_copy(
                src, dst, top_send.at[t, i], top_recv.at[t, i], device, MESH
            )

        return [
            copy(drug_top.at[p, 1, 0:8, :], tops.at[t, 0], (ax_up, th), 0),
            copy(drug_top.at[p, 2, 0:8, :], tops.at[t, 1], (ax_down, th), 1),
            copy(drug_top.at[p, 3, 15, :], drug_top.at[p, 3, 7, :], (ax, th_up), 2),
            copy(drug_top.at[p, 4, 0, :], drug_top.at[p, 4, 8, :], (ax, th_down), 3),
        ]

    def wall_flux(t, p):
        if t > 0:
            wait_bytes(table.at[t, pl.ds(1, n_th - 1)], table_recv.at[t])
        free_rows = gathered(lambda o, hi: table_at(t, o)[hi : hi + 1, :])
        surface = drug_now[7]
        flux = open_row[...] * (surface - free_rows)
        lowered = {19: drug_now[0] - 0.25 * flux}
        for q in range(20, 26):
            lowered[q] = drug_now[q - 19] - 0.125 * flux
        post = collide_drug(lowered, surface - flux, [speed_top[i] for i in range(3)])
        drug_top[p, 1, 0:8, :] = post[20]
        drug_top[p, 2, 0:8, :] = post[21]
        drug_top[p, 3, 8:16, :] = post[22]
        drug_top[p, 4, 0:8, :] = post[23]
        for copy in top_copies(t, p):
            copy.start()
        drug_top[p, 0, 0:8, :] = post[19]
        drug_top[p, 5, 0:8, :] = post[24]
        own(p, 25, top)[...] = post[25]

    def wall_first(t, send):
        if t > 0:
            wait_bytes(sums.at[1, t, pl.ds(1, n_th - 1)], sums_recv.at[t])
        total = sums_at(t, 0)[...]
        for o in range(1, n_th):
            total = total + sums_at(t, o)[...]
        flux = line_open[...] * (total - line_count[...] * table_at(t, 0)[...])
        from_lines = flux + RELEASE_RATE * line_strut[...]
        source[...] = from_lines
        if send:
            x = response[0] + response[1] * from_lines
            b = response[2] + response[3] * from_lines
            x, _ = react(x, b, on_wide[0:1, :], off_wide[0:1, :])
            table[t + 1, 0] = x
            for o in far_first:
                table_copy(t + 1, o).start()
        for c in range(8):
            part = pl.ds(128 * c, 128)
            x = propagated[:, part] + from_source[...] * source[c : c + 1, :]
            x, b = react(x, bound[:, part], on_wide[...], off_wide[...])
            substep[:, part] = x
            bound[:, part] = b

    def respond():
        for c in range(8):
            part = pl.ds(128 * c, 128)
            x, b = propagated[:, part], bound[:, part]
            left = 1.0 - on_wide[...] * (1.0 - b)
            still_free = to_surface[...] * (x * left + off_wide[...] * b)
            row = pl.ds(c, 1)
            response[0, row, :] = jnp.sum(still_free, axis=0, keepdims=True)
            response[1, row, :] = jnp.sum(through[...] * left, axis=0, keepdims=True)
            on, off, x, b = on_wide[0:1, :], off_wide[0:1, :], x[0:1, :], b[0:1, :]
            response[2, row, :] = react(x, b, on, off)[1]
            response[3, row, :] = on * from_source[0:1, :] * (1.0 - b)

    def wall_second():
        wide_on = jnp.concatenate([on_wide[...]] * (WIDTH // 128), axis=1)
        wide_off = jnp.concatenate([off_wide[...]] * (WIDTH // 128), axis=1)
        for c in range(0, n_lines, WIDTH):
            part = pl.ds(c, WIDTH)
            x, b = react(diffuse(wide, substep[:, part]), bound[:, part], wide_on, wide_off)
            bound[:, part] = b
            propagated[:, part] = diffuse(wide, x)

    def top_moved(t, p):
        f = {19: drug_top[p, 0, 0:8, :]}
        f[20] = jnp.where(lane == 0, pltpu.roll(tops[t, 0], 1, 1), pltpu.roll(drug_top[p, 1, 0:8, :], 1, 1))
        f[21] = jnp.where(lane == 127, pltpu.roll(tops[t, 1], 127, 1), pltpu.roll(drug_top[p, 2, 0:8, :], 127, 1))
        f[22] = drug_top[p, 3, 7:15, :]
        f[23] = drug_top[p, 4, 1:9, :]
        f[24] = own(p, 24, top - 1)[...]
        f[25] = drug_top[p, 5, 0:8, :]
        total = f[19]
        for q in range(20, 26):
            total = total + f[q]
        return f, total

    def wait_tops(t, p):
        for copy in top_copies(t, p):
            copy.wait()

    def wait_flow(t, p):
        wait_edges(t)
        for copy in flow_copies(t, p):
            copy.wait()

    def wait_coupling_sends(t):
        if t == 0:
            wait_bytes(first_in.at[pl.ds(1, n_th - 1)], first_send)
            return
        wait_bytes(table.at[t, pl.ds(1, n_th - 1)], table_send.at[t])
        wait_bytes(sums.at[1, t, pl.ds(1, n_th - 1)], sums_send.at[t])

    through[...] = to_surface[...] * from_source[...]
    collide_all(0, 0)
    respond()
    wait_bytes(first_in.at[pl.ds(1, n_th - 1)], first_recv)
    line_strut[...] = strut_own
    line_open[...] = PERMEABILITY * (1.0 - strut_own)
    count = first_out[0, 1]
    for o in range(1, n_th):
        count = count + first_in[o, 1]
    line_count[...] = count
    covered = gathered(lambda o, hi: (first_in if o else first_out)[o, 0, hi : hi + 1, :])
    open_row[...] = PERMEABILITY * (1.0 - covered)

    def wall_side(t, p):
        wait_tops(t, p)
        f, total = top_moved(t, p)
        for q in range(19, 26):
            drug_now[q - 19] = f[q]
        drug_now[7] = total
        send_sums(t + 1, total)

    for t in range(STEPS - 1):
        p = t % 2
        wall_flux(t, p)
        if p == 1:
            wait_flow(t, p)
            collide_all(t + 1, 1 - p)
        wall_first(t, True)
        if p == 1:
            wall_side(t, p)
        wall_second()
        wait_coupling_sends(t)
        if p == 0:
            wait_flow(t, p)
            collide_all(t + 1, 1 - p)
            wall_side(t, p)
        if t < STEPS - 2:
            respond()

    t, p = STEPS - 1, (STEPS - 1) % 2
    wall_flux(t, p)
    wait_flow(t, p)

    def results(rows):
        for r, where in rows:
            flow = None
            for q in Z_UP[:5]:
                term = moved(p, q, r, where) - moved(p, OPPOSITE[q], r, where)
                flow = term if flow is None else flow + term
            axial_out[r] = flow
            if where != "top":
                total = moved(p, 19, r, where)
                for q in range(20, 26):
                    total = total + moved(p, q, r, where)
                drug_out[r] = total

    def results_pair(i, carry):
        results([(2 * i + 1, "middle"), (2 * i + 2, "middle")])
        return carry

    spread_faces(t)
    results([(0, "bottom"), (top, "top")])
    lax.fori_loop(0, (top - 1) // 2, results_pair, 0)
    wall_first(t, False)
    wait_coupling_sends(t)
    wait_tops(t, p)
    drug_out[top] = top_moved(t, p)[1]


def finish(
    substep, bound_in, wide, on_wide, off_wide, drug_in, axial_in,
    drug, axial, free, bound,
    free_part, bound_part, sems,
):
    copies = [
        pltpu.make_async_copy(drug_in, drug, sems.at[0]),
        pltpu.make_async_copy(axial_in, axial, sems.at[1]),
    ]
    for copy in copies:
        copy.start()
    wide_on = jnp.concatenate([on_wide[...]] * (WIDTH // 128), axis=1)
    wide_off = jnp.concatenate([off_wide[...]] * (WIDTH // 128), axis=1)
    for i in range(substep.shape[1] // WIDTH):
        part = pl.ds(i * WIDTH, WIDTH)
        x, b = react(diffuse(wide, substep[:, part]), bound_in[:, part], wide_on, wide_off)
        free_part[:, part] = x
        bound_part[:, part] = b
        for k, (src, dst) in enumerate(((free_part, free), (bound_part, bound))):
            copy = pltpu.make_async_copy(src.at[:, part], dst.at[:, part], sems.at[2 + 2 * i + k])
            copy.start()
            copies.append(copy)
    for copy in copies:
        copy.wait()


def per_device(
    populations, wall_free, wall_bound, wall_propagator, bind_on, bind_off,
    iface_sector, iface_line, strut_mask,
):
    n_th = lax.axis_size("th")
    radial = populations.shape[1]
    vmem = pl.BlockSpec(memory_space=pltpu.VMEM)
    hbm = pl.BlockSpec(memory_space=pltpu.HBM)
    block = (8, 128)
    wall_block = pltpu.VMEM(wall_free.shape, F32)
    scratch = [
        pltpu.VMEM(populations.shape, F32),
        wall_block,
        pltpu.VMEM((128, 128), F32),
        pltpu.VMEM((1, 128), F32),
        pltpu.VMEM((1, 128), F32),
        pltpu.VMEM(block, jnp.int32),
        pltpu.VMEM(block, jnp.int32),
        pltpu.VMEM(block, jnp.int32),
        pltpu.VMEM((7, *block), F32),
        pltpu.VMEM((8, wall_free.shape[1]), F32),
        pltpu.SemaphoreType.DMA((11,)),
        pltpu.VMEM((2, len(MOVING), radial, 16, 128), F32),
        pltpu.VMEM((2, len(STILL), radial, 8, 128), F32),
        pltpu.VMEM((2, 6, 16, 128), F32),
        pltpu.VMEM((8, *block), F32),
        pltpu.VMEM((3, *block), F32),
        pltpu.VMEM((STEPS, 2, *block), F32),
        pltpu.VMEM((STEPS, 2, 24, 128), F32),
        pltpu.VMEM((12, *block), F32),
        pltpu.VMEM((STEPS, 2, *block), F32),
        pltpu.VMEM((8 * n_th, 1024), BF16),
        pltpu.VMEM((128, 1024), BF16),
        pltpu.VMEM(block, jnp.int32),
        pltpu.VMEM(block, jnp.int32),
        pltpu.VMEM(block, F32),
        pltpu.VMEM(block, F32),
        pltpu.VMEM(block, F32),
        pltpu.VMEM(block, F32),
        pltpu.VMEM((STEPS, n_th, *block), F32),
        pltpu.VMEM((2, STEPS, n_th, *block), F32),
        pltpu.VMEM((n_th, 4, *block), F32),
        pltpu.VMEM((n_th, 4, *block), F32),
        pltpu.VMEM(block, F32),
        pltpu.VMEM((128, 128), F32),
        pltpu.VMEM((128, 128), F32),
        pltpu.VMEM((128, 128), F32),
        pltpu.VMEM((4, *block), F32),
        wall_block,
        pltpu.SemaphoreType.DMA((STEPS,)),
        pltpu.SemaphoreType.DMA((STEPS,)),
        pltpu.SemaphoreType.DMA((STEPS,)),
        pltpu.SemaphoreType.DMA((STEPS,)),
        pltpu.SemaphoreType.DMA,
        pltpu.SemaphoreType.DMA,
        pltpu.SemaphoreType.DMA((STEPS, 2)),
        pltpu.SemaphoreType.DMA((STEPS, 2)),
        pltpu.SemaphoreType.DMA((STEPS, 6)),
        pltpu.SemaphoreType.DMA((STEPS, 6)),
        pltpu.SemaphoreType.DMA((STEPS, 4)),
        pltpu.SemaphoreType.DMA((STEPS, 4)),
    ]
    field = jax.ShapeDtypeStruct((radial, *block), F32)
    wall = jax.ShapeDtypeStruct(wall_free.shape, F32)
    square = jax.ShapeDtypeStruct((128, 128), F32)
    drug, axial, substep, bound, wide, on_wide, off_wide = pl.pallas_call(
        kernel,
        out_shape=(
            field, field, wall, wall, jax.ShapeDtypeStruct((128, 384), BF16), square, square,
        ),
        in_specs=[hbm] * 9,
        out_specs=(vmem,) * 7,
        scratch_shapes=scratch,
        compiler_params=pltpu.CompilerParams(
            collective_id=0, has_side_effects=True, vmem_limit_bytes=40 * 2**20
        ),
    )(
        *(
            pltpu.with_memory_space_constraint(x, pltpu.HBM)
            for x in (
                populations, wall_free, wall_bound, wall_propagator,
                bind_on.reshape(1, 128), bind_off.reshape(1, 128),
                iface_sector.reshape(block), iface_line.reshape(block), strut_mask.reshape(block),
            )
        )
    )
    return pl.pallas_call(
        finish,
        out_shape=(field, field, wall, wall),
        in_specs=[vmem] * 7,
        out_specs=(hbm,) * 4,
        scratch_shapes=[
            wall_block,
            wall_block,
            pltpu.SemaphoreType.DMA((2 + 2 * (wall_free.shape[1] // WIDTH),)),
        ],
        compiler_params=pltpu.CompilerParams(vmem_limit_bytes=16 * 2**20),
    )(substep, bound, wide, on_wide, off_wide, drug, axial)


def solution(mesh):
    cells = P(None, "th", "ax")
    lines = P(None, ("ax", "th"))
    return jax.shard_map(
        per_device,
        mesh=mesh,
        in_specs=(
            P(None, None, "th", "ax"), lines, lines, P(), P(), P(),
            P(("ax", "th"), None), P(("ax", "th")), P(("ax", "th")),
        ),
        out_specs=(cells, cells, lines, lines),
        check_vma=False,
    )
```
